128 devices in a mesh: seg: 32 (over y, z, core), sub: 4 (over x).
Axes of the slice: x: 4, y: 4, z: 4, core: 2. Of those that a mesh axis runs over, the one named last changes fastest.
Arguments:
- populations: float32 [2560, 19, 4096], P(('seg', 'sub')), as said below
- neighbours: int32 [2560, 18], P(('seg', 'sub')), may hold values from -1 to 2559, as said below
- site_flags: int32 [2560, 4096], P(('seg', 'sub')), may hold values from 0 to 3, as said below
Outputs:
- populations_out: float32 [2560, 19, 4096], P(('seg', 'sub'))
The draws below stay inside these ranges and needn't reach their ends.
Inputs may be any that keep to these rules, and one draw needn't show every extreme that they name: `populations`: every entry is positive. `neighbours`: -1 marks an absent brick. Otherwise the named brick lies at most 20 places from this brick along the brick order, and its entry in the opposite direction names this brick. `site_flags`: 0 fluid, 1 wall, 2 inlet, 3 outlet; every kind occurs.
All inputs are finite; a program needn't handle non-finite values.
Results may differ from the reference program's by a relative error of at most 0.0003.
Values sent between devices are 32-bit elements; how exact they have to be, the bound alone decides.
No kernel may reach another device: no remote copies, remote signals or barrier semaphores. Data moves between devices by JAX's collectives and lax.ppermute only.
A program may use at most 256 MiB of HBM per device.

```python
import jax
import jax.numpy as jnp
import numpy as np
from jax import lax

BRICK = 16
ACROSS = 4
BRICKS_DEV = 20
STEPS = 2
SITES = 4096
BRICKS = 2560
SLABS = 200
N_SEG = 32
N_SUB = 4


def brick_geometry(key):
    places = SLABS * ACROSS * ACROSS
    guarded = 2 * ACROSS * ACROSS
    dropped = places - BRICKS
    shuffled = jax.random.permutation(jax.random.fold_in(key, 11), places - 2 * guarded)
    removed = jnp.zeros((places,), jnp.int32).at[shuffled[:dropped] + guarded].set(1)
    active = 1 - removed
    ranking = jnp.cumsum(active) - 1
    lookup = jnp.where(active == 1, ranking, -1).astype(jnp.int32)
    positions = jnp.nonzero(active, size=BRICKS)[0].astype(jnp.int32)
    return (lookup, positions)


def draw_neighbours(key, part):
    lookup, positions = brick_geometry(key)
    steps_table = jnp.array([[1, 0, 0], [-1, 0, 0], [0, 1, 0], [0, -1, 0], [0, 0, 1], [0, 0, -1], [1, 1, 0], [-1, -1, 0], [1, -1, 0], [-1, 1, 0], [1, 0, 1], [-1, 0, -1], [1, 0, -1], [-1, 0, 1], [0, 1, 1], [0, -1, -1], [0, 1, -1], [0, -1, 1]], jnp.int32)
    slab_of = positions // (ACROSS * ACROSS)
    row_of = positions // ACROSS % ACROSS
    column_of = positions % ACROSS
    target_slab = slab_of[:, None] + steps_table[None, :, 0]
    target_row = row_of[:, None] + steps_table[None, :, 1]
    target_column = column_of[:, None] + steps_table[None, :, 2]
    inside = (target_slab >= 0) & (target_slab < SLABS) & (target_row >= 0) & (target_row < ACROSS) & (target_column >= 0) & (target_column < ACROSS)
    target_place = (target_slab * ACROSS + target_row) * ACROSS + target_column
    found = lookup[jnp.clip(target_place, 0, SLABS * ACROSS * ACROSS - 1)]
    return jnp.where(inside, found, -1).astype(jnp.int32)


def draw_site_flags(key, part):
    lookup, positions = brick_geometry(key)
    key = jax.random.fold_in(key, 5)
    extent = ACROSS * BRICK
    radius_sq = jax.random.randint(key, (SLABS,), (extent * 7 // 10) ** 2, (extent * 19 // 20) ** 2 + 1)
    site_ids = jnp.arange(SITES, dtype=jnp.int32)
    along_axis = site_ids // (BRICK * BRICK)
    across_first = site_ids // BRICK % BRICK
    across_second = site_ids % BRICK
    slab_of = positions // (ACROSS * ACROSS)
    row_of = positions // ACROSS % ACROSS
    column_of = positions % ACROSS
    doubled_first = 2 * (row_of[:, None] * BRICK + across_first[None, :]) - (extent - 1)
    doubled_second = 2 * (column_of[:, None] * BRICK + across_second[None, :]) - (extent - 1)
    distance = doubled_first * doubled_first + doubled_second * doubled_second
    is_wall = distance > radius_sq[slab_of][:, None]
    global_along = slab_of[:, None] * BRICK + along_axis[None, :]
    at_inlet = global_along == 0
    at_outlet = global_along == SLABS * BRICK - 1
    return jnp.where(is_wall, 1, jnp.where(at_inlet, 2, jnp.where(at_outlet, 3, 0))).astype(jnp.int32)


def draw_populations(key, part):
    key = jax.random.fold_in(key, 7)
    subkeys = jax.random.split(key, 3)
    speeds = jnp.array([[0, 0, 0], [1, 0, 0], [-1, 0, 0], [0, 1, 0], [0, -1, 0], [0, 0, 1], [0, 0, -1], [1, 1, 0], [-1, -1, 0], [1, -1, 0], [-1, 1, 0], [1, 0, 1], [-1, 0, -1], [1, 0, -1], [-1, 0, 1], [0, 1, 1], [0, -1, -1], [0, 1, -1], [0, -1, 1]], jnp.float32)
    weights = jnp.array([1.0 / 3.0] + [1.0 / 18.0] * 6 + [1.0 / 36.0] * 12, jnp.float32)
    along_curve = jnp.arange(BRICKS, dtype=jnp.float32) / BRICKS
    density = (1.0 + (along_curve[:, None] - 0.5)) * jax.random.uniform(subkeys[0], (BRICKS, SITES), jnp.float32, 0.9, 1.1)
    velocity_field = jax.random.uniform(subkeys[1], (BRICKS, 3, SITES), jnp.float32, -0.1, 0.1)
    projected = speeds[None, :, 0, None] * velocity_field[:, None, 0, :] + speeds[None, :, 1, None] * velocity_field[:, None, 1, :] + speeds[None, :, 2, None] * velocity_field[:, None, 2, :]
    jitter = jax.random.uniform(subkeys[2], (BRICKS, 19, SITES), jnp.float32, -0.25, 0.25)
    return weights[None, :, None] * density[:, None, :] * (1.0 + 3.0 * projected + jitter)


def setup_inputs(seed: int = 0) -> dict:
    seeds = jax.random.split(jax.random.key(seed), 4)
    populations = draw_populations(jax.random.fold_in(seeds[3], 71), 0)
    neighbours = draw_neighbours(jax.random.fold_in(seeds[3], 71), 0)
    site_flags = draw_site_flags(jax.random.fold_in(seeds[3], 71), 0)
    return dict(populations=populations, neighbours=neighbours, site_flags=site_flags)


inlet_speed = 0.1

def lattice_speeds():
    return [[0, 0, 0], [1, 0, 0], [-1, 0, 0], [0, 1, 0], [0, -1, 0], [0, 0, 1], [0, 0, -1], [1, 1, 0], [-1, -1, 0], [1, -1, 0], [-1, 1, 0], [1, 0, 1], [-1, 0, -1], [1, 0, -1], [-1, 0, 1], [0, 1, 1], [0, -1, -1], [0, 1, -1], [0, -1, 1]]

def lattice_weights():
    return [1.0 / 3.0] + [1.0 / 18.0] * 6 + [1.0 / 36.0] * 12

def opposite_list():
    return [0, 2, 1, 4, 3, 6, 5, 8, 7, 10, 9, 12, 11, 14, 13, 16, 15, 18, 17]

def relax_matrix():
    speeds = np.array(lattice_speeds()) * 1.0
    along_x = speeds[:, 0]
    along_y = speeds[:, 1]
    along_z = speeds[:, 2]
    monomials = [np.ones(19), along_x, along_y, along_z, along_x * along_x, along_y * along_y, along_z * along_z, along_x * along_y, along_x * along_z, along_y * along_z, along_x * along_x * along_y, along_x * along_x * along_z, along_y * along_y * along_x, along_y * along_y * along_z, along_z * along_z * along_x, along_z * along_z * along_y, along_x * along_x * along_y * along_y, along_x * along_x * along_z * along_z, along_y * along_y * along_z * along_z]
    orthonormal = []
    for vector in monomials:
        for earlier in orthonormal:
            vector = vector - np.dot(vector, earlier) * earlier
        orthonormal.append(vector / np.sqrt(np.dot(vector, vector)))
    moments = np.stack(orthonormal)
    rate_list = np.array([0.0] * 4 + [1.6] * 6 + [1.2] * 6 + [1.4] * 3)
    return np.dot(moments.T * rate_list[None, :], moments)

def face_members():
    speeds = np.array(lattice_speeds())
    members = []
    for face_id in range(6):
        normal = speeds[face_id + 1]
        members.append([member for member in range(19) if int(np.dot(speeds[member], normal)) == 1])
    return members

def equilibrium(density, velocity_field):
    speeds = jnp.asarray(lattice_speeds(), dtype=jnp.float32)
    weights = jnp.asarray(lattice_weights(), dtype=jnp.float32)
    projected = jnp.einsum('ic,bcs->bis', speeds, velocity_field, precision=lax.Precision.HIGHEST)
    square = lax.optimization_barrier(jnp.sum(velocity_field * velocity_field, axis=1))[:, None, :]
    return weights[None, :, None] * density[:, None, :] * (1.0 + 3.0 * projected + 4.5 * projected * projected - 1.5 * square)

def collide(states, density, site_kinds, mean_density):
    speeds = jnp.asarray(lattice_speeds(), dtype=jnp.float32)
    momentum = jnp.einsum('ic,bis->bcs', speeds, states, precision=lax.Precision.HIGHEST)
    velocity_field = momentum / density[:, None, :]
    relaxation = jnp.asarray(relax_matrix(), dtype=jnp.float32)
    relaxed = states - jnp.einsum('ij,bjs->bis', relaxation, states - equilibrium(density, velocity_field), precision=lax.Precision.HIGHEST)
    bounced = states[:, np.array(opposite_list()), :]
    inflow = equilibrium(density, jnp.zeros_like(velocity_field).at[:, 0, :].set(inlet_speed))
    outflow = equilibrium(jnp.zeros_like(density) + mean_density, velocity_field)
    flag_rows = site_kinds[:, None, :]
    return jnp.where(flag_rows == 1, bounced, jnp.where(flag_rows == 2, inflow, jnp.where(flag_rows == 3, outflow, relaxed)))

def layer_table(states):
    bricks = states.shape[0]
    brick_cube = states.reshape(bricks, 19, BRICK, BRICK, BRICK)
    face_layers = []
    for face_id, members in enumerate(face_members()):
        dimension = face_id // 2
        position = BRICK - 1 if face_id % 2 == 0 else 0
        chosen = brick_cube[:, np.array(members)]
        sheet_out = lax.index_in_dim(chosen, position, dimension + 2, keepdims=False)
        face_layers.append(sheet_out.reshape(bricks, 5, BRICK * BRICK))
    return jnp.stack(face_layers, axis=1)

def place_at(shifted, values, dims_list, targets):
    indexer = [slice(None)] * 4
    for dimension, target in zip(dims_list, targets):
        indexer[dimension + 1] = target
    return shifted.at[tuple(indexer)].set(values)

def take_at(mirror, dims_list, targets):
    indexer = [slice(None)] * 4
    for dimension, target in zip(dims_list, targets):
        indexer[dimension + 1] = target
    return mirror[tuple(indexer)]

def stream(posted, rim_table, source, absent):
    bricks = posted.shape[0]
    brick_cube = posted.reshape(bricks, 19, BRICK, BRICK, BRICK)
    speeds = lattice_speeds()
    opposite = opposite_list()
    members = face_members()
    outputs = [brick_cube[:, 0]]
    for member in range(1, 19):
        stride = speeds[member]
        shifted = jnp.roll(brick_cube[:, member], tuple(stride), axis=(1, 2, 3))
        mirror = brick_cube[:, opposite[member]]
        crossed = [dimension for dimension in range(3) if stride[dimension] != 0]
        for dimension in crossed:
            heading = stride[dimension]
            toward = 2 * dimension + (1 if heading > 0 else 0)
            face_id = 2 * dimension + (0 if heading > 0 else 1)
            slot_id = members[face_id].index(member)
            incoming = rim_table[source[:, toward], face_id, slot_id].reshape(bricks, BRICK, BRICK)
            others = [other for other in range(3) if other != dimension]
            incoming = jnp.roll(incoming, (stride[others[0]], stride[others[1]]), axis=(1, 2))
            target = 0 if heading > 0 else BRICK - 1
            fallback = take_at(mirror, [dimension], [target])
            incoming = jnp.where(absent[:, toward][:, None, None], fallback, incoming)
            shifted = place_at(shifted, incoming, [dimension], [target])
        if len(crossed) == 2:
            leading, second = crossed
            toward = opposite[member] - 1
            face_id = 2 * leading + (0 if stride[leading] > 0 else 1)
            slot_id = members[face_id].index(member)
            incoming = rim_table[source[:, toward], face_id, slot_id].reshape(bricks, BRICK, BRICK)
            others = [other for other in range(3) if other != leading]
            edge_place = BRICK - 1 if stride[second] > 0 else 0
            edge_line = lax.index_in_dim(incoming, edge_place, others.index(second) + 1, keepdims=False)
            targets = [0 if stride[leading] > 0 else BRICK - 1, 0 if stride[second] > 0 else BRICK - 1]
            fallback = take_at(mirror, [leading, second], targets)
            edge_line = jnp.where(absent[:, toward][:, None], fallback, edge_line)
            shifted = place_at(shifted, edge_line, [leading, second], targets)
        outputs.append(shifted)
    return jnp.stack(outputs, axis=1).reshape(bricks, 19, BRICK * BRICK * BRICK)

def reference(populations, neighbours, site_flags):
    groups = N_SEG * N_SUB
    absent = neighbours < 0
    source = jnp.where(absent, 0, neighbours).astype(jnp.int32)
    flags_grouped = site_flags.reshape(groups, BRICKS_DEV, SITES)
    source_grouped = source.reshape(groups, BRICKS_DEV, 18)
    absent_grouped = absent.reshape(groups, BRICKS_DEV, 18)
    current = populations
    for repeat in range(STEPS):
        density = lax.optimization_barrier(jnp.sum(current, axis=1))
        fluid_sites = site_flags != 1
        mean_density = jnp.sum(jnp.where(fluid_sites, density, 0.0)) / jnp.sum(fluid_sites.astype(jnp.float32))
        grouped = current.reshape(groups, BRICKS_DEV, 19, SITES)

        def rims_of(pieces):
            states, site_kinds = pieces
            return layer_table(collide(states, lax.optimization_barrier(jnp.sum(states, axis=1)), site_kinds, mean_density))
        rim_table = lax.map(rims_of, (grouped, flags_grouped)).reshape(BRICKS, 6, 5, BRICK * BRICK)

        def advance(pieces):
            states, site_kinds, rows_from, missing = pieces
            posted = collide(states, lax.optimization_barrier(jnp.sum(states, axis=1)), site_kinds, mean_density)
            return stream(posted, rim_table, rows_from, missing)
        current = lax.map(advance, (grouped, flags_grouped, source_grouped, absent_grouped)).reshape(BRICKS, 19, SITES)
    return current
```

```python
import functools

import jax
import jax.numpy as jnp
import numpy as np
from jax import lax
from jax.experimental import pallas as pl
from jax.experimental.pallas import tpu as pltpu
from jax.sharding import PartitionSpec as P

BRICK = 16
PLANE = 256
SITES = 4096
GROUP = 4
AXES = ("seg", "sub")
INLET = 0.1

SPEEDS = [
    (0, 0, 0),
    (1, 0, 0), (-1, 0, 0), (0, 1, 0), (0, -1, 0), (0, 0, 1), (0, 0, -1),
    (1, 1, 0), (-1, -1, 0), (1, -1, 0), (-1, 1, 0),
    (1, 0, 1), (-1, 0, -1), (1, 0, -1), (-1, 0, 1),
    (0, 1, 1), (0, -1, -1), (0, 1, -1), (0, -1, 1),
]
OPP = [0, 2, 1, 4, 3, 6, 5, 8, 7, 10, 9, 12, 11, 14, 13, 16, 15, 18, 17]


def face_of(speed, dim):
    return 2 * dim + (0 if speed[dim] > 0 else 1)


MEMBERS = [[i for i in range(19) if any(face_of(SPEEDS[i], d) == f and SPEEDS[i][d] for d in range(3))]
           for f in range(6)]
COLUMN_FACE = []
for _d in range(18):
    _m = SPEEDS[OPP[_d + 1]]
    _lead = [k for k in range(3) if _m[k]][0]
    COLUMN_FACE.append(face_of(_m, _lead))


def iota(shape, dim):
    return lax.broadcasted_iota(jnp.int32, shape, dim)


def roll(x, shift, axis):
    shift = shift % x.shape[axis]
    return x if shift == 0 else pltpu.roll(x, shift, axis)


def collide(f, kind, mean):
    fluid = kind == 0
    wall = kind == 1
    inlet = kind == 2
    outlet = kind == 3
    even = [f[2 * k + 1] + f[2 * k + 2] for k in range(9)]
    odd = [f[2 * k + 1] - f[2 * k + 2] for k in range(9)]
    density = f[0] + ((even[0] + even[1]) + (even[2] + even[3])) + (
        (even[4] + even[5]) + (even[6] + even[7])) + even[8]
    inverse = 1.0 / density
    ux = (odd[0] + odd[3] + odd[4] + odd[5] + odd[6]) * inverse
    uy = (odd[1] + odd[3] - odd[4] + odd[7] + odd[8]) * inverse
    uz = (odd[2] + odd[5] - odd[6] + odd[7] - odd[8]) * inverse
    ux = jnp.where(inlet, INLET, ux)
    uy = jnp.where(inlet, 0.0, uy)
    uz = jnp.where(inlet, 0.0, uz)
    rho = jnp.where(outlet, mean, density)
    base = 1.0 - 1.5 * (ux * ux + uy * uy + uz * uz)
    along = [ux, uy, uz, ux + uy, ux - uy, ux + uz, ux - uz, uy + uz, uy - uz]
    keep_even = jnp.where(fluid, -0.3, jnp.where(wall, 0.5, 0.0))
    take_even = jnp.where(fluid, 0.8, jnp.where(wall, 0.0, 0.5))
    keep_odd = jnp.where(fluid, -0.1, jnp.where(wall, -0.5, 0.0))
    take_odd = jnp.where(fluid, 0.6, jnp.where(wall, 0.0, 0.5))
    fourth = jnp.where(fluid, 0.2 / 12.0, 0.0)
    rho9 = rho * (1.0 / 9.0)
    rho18 = rho * (1.0 / 18.0)
    eq_even = []
    for k in range(9):
        scale = rho9 if k < 3 else rho18
        eq_even.append(scale * (base + 4.5 * along[k] * along[k]))
    eq_rest = (rho * (1.0 / 3.0)) * base
    g_rest = f[0] - eq_rest
    g = [even[k] - eq_even[k] for k in range(9)]
    four = 4.0 * g_rest
    gx, gy, gz = 2.0 * g[0], 2.0 * g[1], 2.0 * g[2]
    ta = four - gx - gy + (g[3] + g[4])
    tb = four - gx - gz + (g[5] + g[6])
    tc = four - gy - gz + (g[7] + g[8])
    shared = (2.0 / 7.0) * (ta + tb + tc)
    ka = (ta - shared) * fourth
    kb = (tb - shared) * fourth
    kc = (tc - shared) * fourth
    kab, kac, kbc = ka + kb, ka + kc, kb + kc
    modes = [-2.0 * kab, -2.0 * kac, -2.0 * kbc, ka, ka, kb, kb, kc, kc]
    odd9 = rho * take_odd * (1.0 / 3.0)
    odd18 = rho * take_odd * (1.0 / 6.0)
    out = [2.0 * (keep_even * f[0] + take_even * eq_rest) + 4.0 * (kab + kc)]
    for k in range(9):
        half_even = keep_even * even[k] + take_even * eq_even[k] + modes[k]
        half_odd = keep_odd * odd[k] + (odd9 if k < 3 else odd18) * along[k]
        out.append(half_even + half_odd)
        out.append(half_even - half_odd)
    return out, density


def cyclic(halves, speed):
    lane = iota((BRICK, 128), 1)
    cx, cy, cz = speed
    low, high = halves
    if cx:
        low, high = roll(low, cx, 0), roll(high, cx, 0)
    if cy:
        first, second = roll(low, 16 * cy, 1), roll(high, 16 * cy, 1)
        carried = lane < 16 if cy > 0 else lane >= 112
        low, high = jnp.where(carried, second, first), jnp.where(carried, first, second)
    if cz:
        wrapped = (lane & 15) == (0 if cz > 0 else 15)
        low = jnp.where(wrapped, roll(low, -15 * cz, 1), roll(low, cz, 1))
        high = jnp.where(wrapped, roll(high, -15 * cz, 1), roll(high, cz, 1))
    return low, high


def pack_faces(table, row, values):
    lane = iota((BRICK, 128), 1)
    for face in range(6):
        dim = face // 2
        place = 0 if face % 2 == 0 else 15
        packed = None
        for slot, member in enumerate(MEMBERS[face]):
            low, high = values(member, face)
            if dim == 0:
                table[row, face, slot:slot + 1, :] = low[place:place + 1, :]
                table[row, face, 8 + slot:9 + slot, :] = high[place:place + 1, :]
            elif dim == 1:
                piece = low if place == 0 else high
                moved = roll(piece, 16 * slot - (0 if place == 0 else 112), 1)
                packed = moved if packed is None else jnp.where((lane >> 4) == slot, moved, packed)
            else:
                first, second = roll(low, slot - place, 1), roll(high, 8 + slot - place, 1)
                packed = first if packed is None else jnp.where((lane & 15) == slot, first, packed)
                packed = jnp.where((lane & 15) == 8 + slot, second, packed)
        if dim != 0:
            table[row, face] = packed


def shift_and_pack(posted, q, moved, faces, mirrors):
    def halves(member):
        return posted[member, :, 0:128], posted[member, :, 128:256]

    for member in range(19):
        low, high = cyclic(halves(member), SPEEDS[member])
        moved[q, member, :, 0:128] = low
        moved[q, member, :, 128:256] = high
    pack_faces(faces, q, lambda m, face: (moved[q, m, :, 0:128], moved[q, m, :, 128:256]))
    pack_faces(mirrors, q, lambda m, face: halves(OPP[m]))


def arrive(moved, q, member, table, source):
    lane = iota((BRICK, 128), 1)
    sub = iota((BRICK, 128), 0)
    speed = SPEEDS[member]
    cx, cy, cz = speed
    parts = [moved[q, member, :, 0:128], moved[q, member, :, 128:256]]

    def column(dim):
        return 2 * dim + (1 if speed[dim] > 0 else 0)

    edge = OPP[member] - 1
    if cy:
        face = face_of(speed, 1)
        slot = MEMBERS[face].index(member)
        place = 0 if cy > 0 else 15
        half = place // 8
        shift = (0 if place == 0 else 112) - 16 * slot
        here = (lane >> 4) == place % 8
        block = table[source(column(1))]
        if cz:
            corner = here & ((lane & 15) == (0 if cz > 0 else 15))
        parts[half] = jnp.where(here, roll(block, shift, 1), parts[half])
    if cz:
        face = face_of(speed, 2)
        slot = MEMBERS[face].index(member)
        place = 0 if cz > 0 else 15
        here = (lane & 15) == place
        block = table[source(column(2))]
        parts[0] = jnp.where(here, roll(block, place - slot, 1), parts[0])
        parts[1] = jnp.where(here, roll(block, place - slot - 8, 1), parts[1])
    if cy and cz:
        face = face_of(speed, 1)
        slot = MEMBERS[face].index(member)
        place = 0 if cy > 0 else 15
        shift = (0 if place == 0 else 112) - 16 * slot
        half = place // 8
        parts[half] = jnp.where(corner, roll(table[source(edge)], shift, 1), parts[half])
    if cx:
        face = face_of(speed, 0)
        slot = MEMBERS[face].index(member)
        place = 0 if cx > 0 else 15
        row_lane = iota((1, 128), 1)
        for half in range(2):
            line = table[source(column(0)), 8 * half + slot:8 * half + slot + 1, :]
            spot = None
            if cy:
                across = 0 if cy > 0 else 15
                if across // 8 == half:
                    spot = (row_lane >> 4) == across % 8
            elif cz:
                spot = (row_lane & 15) == (0 if cz > 0 else 15)
            if spot is not None:
                other = table[source(edge), 8 * half + slot:8 * half + slot + 1, :]
                line = jnp.where(spot, other, line)
            parts[half] = jnp.where(sub == place, jnp.broadcast_to(line, (BRICK, 128)), parts[half])
    return parts


def mean_of(gathered):
    total = jnp.sum(gathered[...], axis=0, keepdims=True)
    ratio = total / pltpu.roll(total, 64, 1)
    return jnp.broadcast_to(ratio[:, 0:1], (8, 128))


def collide_brick(load, kinds, q, posted, mean):
    for g in range(2):
        for h in range(2):
            rows, lanes = slice(8 * g, 8 * g + 8), slice(128 * h, 128 * h + 128)
            f = [load(i, g, h) for i in range(19)]
            out, _ = collide(f, kinds[q, rows, lanes], mean)
            for i in range(19):
                posted[i, rows, lanes] = out[i]


def first_kernel(gathered, pops, kinds, moved, faces, mirrors, tiles, posted):
    mean = mean_of(gathered)

    def brick(q, carry):
        for r in range(3):
            high = 8 if r < 2 else 3
            for c in range(32):
                start = (r * 32 + c) * 8
                tiles[start:start + high, :] = pops[q, 8 * r:8 * r + high, 128 * c:128 * c + 128]

        def load(i, g, h):
            start = ((i // 8) * 32 + 16 * g + h) * 8 + i % 8
            return tiles[pl.ds(start, 8, stride=16), :]

        collide_brick(load, kinds, q, posted, mean)
        shift_and_pack(posted, q, moved, faces, mirrors)
        return carry

    lax.fori_loop(0, GROUP, brick, 0)


def later_kernel(gathered, pops, kinds, moved, faces, mirrors, posted):
    mean = mean_of(gathered)

    def brick(q, carry):
        def load(i, g, h):
            return pops[q, i, 8 * g:8 * g + 8, 128 * h:128 * h + 128]

        collide_brick(load, kinds, q, posted, mean)
        shift_and_pack(posted, q, moved, faces, mirrors)
        return carry

    lax.fori_loop(0, GROUP, brick, 0)


def fill_table(pieces, table, sems):
    copies = []
    start = 0
    for k, piece in enumerate(pieces):
        count = piece.shape[0]
        copies.append(pltpu.make_async_copy(piece, table.at[pl.ds(start, count)], sems.at[k]))
        start += count
    for copy in copies:
        copy.start()
    for copy in copies:
        copy.wait()


def arrive_sum_kernel(index, moved, kinds, own, mirror, even, odd, pops, sums, table, sems):
    step = pl.program_id(0)

    @pl.when(step == 0)
    def _():
        fill_table((own, mirror, even, odd), table, sems)
        sums[...] = jnp.zeros_like(sums)

    def brick(q, carry):
        base = (step * GROUP + q) * 18
        source = lambda column: index[base + column]
        total = [None, None]
        for member in range(19):
            parts = arrive(moved, q, member, table, source)
            for h in range(2):
                pops[q, member, :, 128 * h:128 * h + 128] = parts[h]
                total[h] = parts[h] if total[h] is None else total[h] + parts[h]
        for h in range(2):
            open_site = kinds[q, :, 128 * h:128 * h + 128] != 1
            sums[0] += jnp.where(open_site, total[h], 0.0)
            sums[1] += jnp.where(open_site, 1.0, 0.0)
        return carry

    lax.fori_loop(0, GROUP, brick, 0)


def arrive_out_kernel(index, moved, own, mirror, even, odd, out, table, tiles, sems):
    step = pl.program_id(0)

    @pl.when(step == 0)
    def _():
        fill_table((own, mirror, even, odd), table, sems)

    def brick(q, carry):
        base = (step * GROUP + q) * 18
        source = lambda column: index[base + column]
        for member in range(19):
            parts = arrive(moved, q, member, table, source)
            for g in range(2):
                for h in range(2):
                    start = ((member // 8) * 32 + 16 * g + h) * 8 + member % 8
                    tiles[pl.ds(start, 8, stride=16), :] = parts[h][8 * g:8 * g + 8, :]
        for r in range(3):
            high = 8 if r < 2 else 3
            for c in range(32):
                start = (r * 32 + c) * 8
                out[q, 8 * r:8 * r + high, 128 * c:128 * c + 128] = tiles[start:start + high, :]
        return carry

    lax.fori_loop(0, GROUP, brick, 0)


def params():
    return pltpu.CompilerParams(
        dimension_semantics=("arbitrary",), vmem_limit_bytes=48 * 1024 * 1024)


def brick_spec(*shape):
    return pl.BlockSpec((GROUP,) + shape, lambda i: (i,) + (0,) * len(shape))


def whole_spec(*shape):
    return pl.BlockSpec(shape, lambda i: (0,) * len(shape))


MOVED = (19, BRICK, PLANE)
LAYERS = (6, BRICK, 128)
F32 = jnp.float32


def collide_call(gathered, pops, kinds, native):
    bricks = pops.shape[0]
    scratch = [pltpu.VMEM((768, 128), F32)] if native else []
    return pl.pallas_call(
        first_kernel if native else later_kernel,
        grid=(bricks // GROUP,),
        in_specs=[whole_spec(*gathered.shape),
                  brick_spec(19, SITES) if native else brick_spec(*MOVED),
                  brick_spec(BRICK, PLANE)],
        out_specs=[brick_spec(*MOVED), brick_spec(*LAYERS), brick_spec(*LAYERS)],
        out_shape=[jax.ShapeDtypeStruct((bricks,) + MOVED, F32),
                   jax.ShapeDtypeStruct((bricks,) + LAYERS, F32),
                   jax.ShapeDtypeStruct((bricks,) + LAYERS, F32)],
        scratch_shapes=scratch + [pltpu.VMEM(MOVED, F32)],
        compiler_params=params(),
        name="collide_shift",
    )(gathered, pops, kinds)


def table_rows(pieces):
    return sum(piece.shape[0] for piece in pieces)


def arrive_sum_call(index, moved, kinds, pieces):
    bricks = moved.shape[0]
    anywhere = pl.BlockSpec(memory_space=pl.ANY)
    return pl.pallas_call(
        arrive_sum_kernel,
        grid=(bricks // GROUP,),
        in_specs=[pl.BlockSpec(memory_space=pltpu.SMEM), brick_spec(*MOVED),
                  brick_spec(BRICK, PLANE)] + [anywhere] * 4,
        out_specs=[brick_spec(*MOVED), whole_spec(2, BRICK, 128)],
        out_shape=[jax.ShapeDtypeStruct((bricks,) + MOVED, F32),
                   jax.ShapeDtypeStruct((2, BRICK, 128), F32)],
        scratch_shapes=[pltpu.VMEM((table_rows(pieces), BRICK, 128), F32),
                        pltpu.SemaphoreType.DMA((4,))],
        compiler_params=params(),
        name="arrive_sum",
    )(index, moved, kinds, *pieces)


def arrive_out_call(index, moved, pieces):
    bricks = moved.shape[0]
    anywhere = pl.BlockSpec(memory_space=pl.ANY)
    return pl.pallas_call(
        arrive_out_kernel,
        grid=(bricks // GROUP,),
        in_specs=[pl.BlockSpec(memory_space=pltpu.SMEM), brick_spec(*MOVED)] + [anywhere] * 4,
        out_specs=brick_spec(19, SITES),
        out_shape=jax.ShapeDtypeStruct((bricks, 19, SITES), F32),
        scratch_shapes=[pltpu.VMEM((table_rows(pieces), BRICK, 128), F32),
                        pltpu.VMEM((768, 128), F32),
                        pltpu.SemaphoreType.DMA((4,))],
        compiler_params=params(),
        name="arrive_out",
    )(index, moved, *pieces)


def gather_sums(summed, counted, devices):
    left = iota((devices, 128), 1) < 64
    rows = jnp.where(left, summed, counted)
    return lax.all_to_all(rows, AXES, 0, 0, tiled=True)


def swap_layers(layers, devices):
    even_pairs = [(i, i ^ 1) for i in range(devices)]
    odd_pairs = [(i, i + 1) for i in range(1, devices - 1, 2)]
    odd_pairs = odd_pairs + [(b, a) for a, b in odd_pairs]
    return lax.ppermute(layers, AXES, even_pairs), lax.ppermute(layers, AXES, odd_pairs)


def on_device(devices, populations, neighbours, site_flags):
    bricks = populations.shape[0]
    blocks = bricks * 6
    kinds = site_flags.reshape(bricks, BRICK, PLANE)
    me = lax.axis_index(AXES)
    local = neighbours - me * bricks
    parity = me % 2
    after = jnp.where(parity == 0, 2 * blocks, 3 * blocks)
    before = jnp.where(parity == 0, 3 * blocks, 2 * blocks)
    brick_id = iota((bricks, 18), 0)
    place = jnp.where(local < 0, before + (local + bricks) * 6,
                      jnp.where(local >= bricks, after + (local - bricks) * 6, local * 6))
    place = jnp.where(neighbours < 0, blocks + brick_id * 6, place)
    index = (place + jnp.asarray(np.array(COLUMN_FACE, np.int32))[None, :]).reshape(-1)

    open_site = (site_flags != 1)[:, None, :]
    summed = jnp.sum(jnp.where(open_site, populations, 0.0))
    counted = jnp.sum((site_flags != 1).astype(F32))
    flat = lambda layers: layers.reshape(blocks, BRICK, 128)

    gathered = gather_sums(summed, counted, devices)
    moved, faces, mirrors = collide_call(gathered, populations, kinds, True)
    pieces = (flat(faces), flat(mirrors)) + swap_layers(flat(faces), devices)
    pops, sums = arrive_sum_call(index, moved, kinds, pieces)
    totals = jnp.sum(sums, axis=(1, 2))
    gathered = gather_sums(totals[0], totals[1], devices)
    moved, faces, mirrors = collide_call(gathered, pops, kinds, False)
    pieces = (flat(faces), flat(mirrors)) + swap_layers(flat(faces), devices)
    return arrive_out_call(index, moved, pieces)


def solution(mesh):
    devices = mesh.shape["seg"] * mesh.shape["sub"]
    in_specs = (P(AXES, None, None), P(AXES, None), P(AXES, None))
    return jax.shard_map(
        functools.partial(on_device, devices), mesh=mesh, in_specs=in_specs,
        out_specs=P(AXES, None, None), check_vma=False)
```

```python
import functools

import jax
import jax.numpy as jnp
import numpy as np
from jax import lax
from jax.experimental import pallas as pl
from jax.experimental.pallas import tpu as pltpu
from jax.sharding import PartitionSpec as P

BRICK = 16
PLANE = 256
SITES = 4096
GROUP = 8
CHUNKS = 32
AXES = ("seg", "sub")
INLET = 0.1

SPEEDS = [
    (0, 0, 0),
    (1, 0, 0), (-1, 0, 0), (0, 1, 0), (0, -1, 0), (0, 0, 1), (0, 0, -1),
    (1, 1, 0), (-1, -1, 0), (1, -1, 0), (-1, 1, 0),
    (1, 0, 1), (-1, 0, -1), (1, 0, -1), (-1, 0, 1),
    (0, 1, 1), (0, -1, -1), (0, 1, -1), (0, -1, 1),
]
OPP = [0, 2, 1, 4, 3, 6, 5, 8, 7, 10, 9, 12, 11, 14, 13, 16, 15, 18, 17]


def face_of(speed, dim):
    return 2 * dim + (0 if speed[dim] > 0 else 1)


MEMBERS = [[i for i in range(19) if any(face_of(SPEEDS[i], d) == f and SPEEDS[i][d] for d in range(3))]
           for f in range(6)]
COLUMN_FACE = []
for _d in range(18):
    _m = SPEEDS[OPP[_d + 1]]
    _lead = [k for k in range(3) if _m[k]][0]
    COLUMN_FACE.append(face_of(_m, _lead))


def iota(shape, dim):
    return lax.broadcasted_iota(jnp.int32, shape, dim)


def roll(x, shift, axis):
    shift = shift % x.shape[axis]
    return x if shift == 0 else pltpu.roll(x, shift, axis)


def collide(f, kind):
    fluid = kind == 0
    wall = kind == 1
    inlet = kind == 2
    outlet = kind == 3
    even = [f[2 * k + 1] + f[2 * k + 2] for k in range(9)]
    odd = [f[2 * k + 1] - f[2 * k + 2] for k in range(9)]
    density = f[0] + ((even[0] + even[1]) + (even[2] + even[3])) + (
        (even[4] + even[5]) + (even[6] + even[7])) + even[8]
    inverse = 1.0 / density
    ux = (odd[0] + odd[3] + odd[4] + odd[5] + odd[6]) * inverse
    uy = (odd[1] + odd[3] - odd[4] + odd[7] + odd[8]) * inverse
    uz = (odd[2] + odd[5] - odd[6] + odd[7] - odd[8]) * inverse
    ux = jnp.where(inlet, INLET, ux)
    uy = jnp.where(inlet, 0.0, uy)
    uz = jnp.where(inlet, 0.0, uz)
    rho = jnp.where(outlet, 1.0, density)
    base = 1.0 - 1.5 * (ux * ux + uy * uy + uz * uz)
    along = [ux, uy, uz, ux + uy, ux - uy, ux + uz, ux - uz, uy + uz, uy - uz]
    keep_even = jnp.where(fluid, -0.3, jnp.where(wall, 0.5, 0.0))
    take_even = jnp.where(fluid, 0.8, jnp.where(wall, 0.0, 0.5))
    keep_odd = jnp.where(fluid, -0.1, jnp.where(wall, -0.5, 0.0))
    take_odd = jnp.where(fluid, 0.6, jnp.where(wall, 0.0, 0.5))
    fourth = jnp.where(fluid, 0.2 / 12.0, 0.0)
    rho9 = rho * (1.0 / 9.0)
    rho18 = rho * (1.0 / 18.0)
    eq_even = []
    for k in range(9):
        scale = rho9 if k < 3 else rho18
        eq_even.append(scale * (base + 4.5 * along[k] * along[k]))
    eq_rest = (rho * (1.0 / 3.0)) * base
    g_rest = f[0] - eq_rest
    g = [even[k] - eq_even[k] for k in range(9)]
    four = 4.0 * g_rest
    gx, gy, gz = 2.0 * g[0], 2.0 * g[1], 2.0 * g[2]
    ta = four - gx - gy + (g[3] + g[4])
    tb = four - gx - gz + (g[5] + g[6])
    tc = four - gy - gz + (g[7] + g[8])
    shared = (2.0 / 7.0) * (ta + tb + tc)
    ka = (ta - shared) * fourth
    kb = (tb - shared) * fourth
    kc = (tc - shared) * fourth
    kab, kac, kbc = ka + kb, ka + kc, kb + kc
    modes = [-2.0 * kab, -2.0 * kac, -2.0 * kbc, ka, ka, kb, kb, kc, kc]
    odd9 = rho * take_odd * (1.0 / 3.0)
    odd18 = rho * take_odd * (1.0 / 6.0)
    out = [2.0 * (keep_even * f[0] + take_even * eq_rest) + 4.0 * (kab + kc)]
    for k in range(9):
        half_even = keep_even * even[k] + take_even * eq_even[k] + modes[k]
        half_odd = keep_odd * odd[k] + (odd9 if k < 3 else odd18) * along[k]
        out.append(half_even + half_odd)
        out.append(half_even - half_odd)
    return out, density


def side(heading):
    return (15, 0) if heading > 0 else (0, 15)


def slot_of(member, dim):
    return MEMBERS[face_of(SPEEDS[member], dim)].index(member)


def toward(member, dim):
    return 2 * dim + (1 if SPEEDS[member][dim] > 0 else 0)


def pack(value, layers, table, step):
    lane = iota((GROUP, 128), 1)
    for face in range(2):
        leave = 15 if face % 2 == 0 else 0
        for slot, member in enumerate(MEMBERS[face]):
            for h in range(2):
                row = (8 * h + slot) * 8
                layers[face, row:row + 8, :] = value(member, 2 * leave + h)

    def line(x, carry):
        rows = pl.ds(pl.multiple_of(8 * x, 8), 8)
        for face in range(2, 6):
            leave = 15 if face % 2 == 0 else 0
            packed = None
            for slot, member in enumerate(MEMBERS[face]):
                if face < 4:
                    piece = value(member, 2 * x + leave // 8)
                    piece = roll(piece, 16 * slot - 16 * (leave % 8), 1)
                    packed = piece if packed is None else jnp.where((lane >> 4) == slot, piece, packed)
                else:
                    for h in range(2):
                        piece = roll(value(member, 2 * x + h), 8 * h + slot - leave, 1)
                        packed = (piece if packed is None
                                  else jnp.where((lane & 15) == 8 * h + slot, piece, packed))
            layers[face, rows, :] = packed
        return carry

    lax.fori_loop(0, BRICK, line, 0)
    for face in range(6):
        for j in range(GROUP):
            table[(step * GROUP + j) * 6 + face] = layers[face, pl.ds(j, BRICK, stride=8), :]


def gather(index, step, table, marks, mean, arriving):
    wide = jnp.concatenate([mean, mean], axis=0)

    def brick(j, carry):
        base = (step * GROUP + j) * 18
        for column in range(18):
            at = index[base + column]
            block = table[at]
            arriving[column, pl.ds(j, BRICK, stride=8), :] = jnp.where(
                marks[at] != 0.0, block * wide, block)
        return carry

    lax.fori_loop(0, GROUP, brick, 0)


def stream(posted, kinds, absent, arriving, mean, put):
    lane = iota((GROUP, 128), 1)

    def scale(chunk):
        lanes = pl.ds(pl.multiple_of(128 * chunk, 128), 128)
        return jnp.where(kinds[:, lanes] == 3, mean, 1.0)

    def line(x, carry):
        before = (x + 15) & 15
        after = (x + 1) & 15
        place = {0: x, 1: before, -1: after}
        scales = {cx: (scale(2 * place[cx]), scale(2 * place[cx] + 1)) for cx in (0, 1, -1)}

        def load(member, cx, h):
            return posted[0, member, 2 * place[cx] + h] * scales[cx][h]

        for member in range(19):
            cx, cy, cz = SPEEDS[member]
            parts = [load(member, cx, h) for h in range(2)]
            mirror = [None, None]
            if cy or cz:
                mirror = [load(OPP[member], 0, h) for h in range(2)]
            if cy:
                first, second = roll(parts[0], 16 * cy, 1), roll(parts[1], 16 * cy, 1)
                carried = lane < 16 if cy > 0 else lane >= 112
                parts = [jnp.where(carried, second, first), jnp.where(carried, first, second)]
            if cz:
                parts = [roll(part, cz, 1) for part in parts]
            rows = pl.ds(pl.multiple_of(8 * place[cx], 8), 8)
            if cy:
                leave, enter = side(cy)
                column = toward(member, 1)
                half = enter // 8
                shift = 16 * (enter % 8) - 16 * slot_of(member, 1)
                here = (lane >> 4) == enter % 8
                new = roll(arriving[column, rows, :], shift + cz, 1)
                new = jnp.where(absent[column] != 0, mirror[half], new)
                parts[half] = jnp.where(here, new, parts[half])
            if cz:
                leave, enter = side(cz)
                column = toward(member, 2)
                slot = slot_of(member, 2)
                gone = absent[column] != 0
                here = (lane & 15) == enter
                block = arriving[column, rows, :]
                for h in range(2):
                    new = roll(block, 16 * cy + enter - slot - 8 * h, 1)
                    if cy and h == (1 if cy > 0 else 0):
                        other = roll(block, 16 * cy + enter - slot - 8 * (1 - h), 1)
                        new = jnp.where(lane < 16 if cy > 0 else lane >= 112, other, new)
                    new = jnp.where(gone, mirror[h], new)
                    parts[h] = jnp.where(here, new, parts[h])
            if cy and cz:
                leave, enter = side(cy)
                column = OPP[member] - 1
                half = enter // 8
                shift = 16 * (enter % 8) - 16 * slot_of(member, 1)
                corner = ((lane >> 4) == enter % 8) & ((lane & 15) == side(cz)[1])
                new = roll(arriving[column, rows, :], shift - 15 * cz, 1)
                new = jnp.where(absent[column] != 0, mirror[half], new)
                parts[half] = jnp.where(corner, new, parts[half])
            for h in range(2):
                put(member, 2 * x + h, parts[h])
        return carry

    lax.fori_loop(0, BRICK, line, 0)

    for member in range(19):
        cx, cy, cz = SPEEDS[member]
        if not cx:
            continue
        leave, enter = side(cx)
        slot = slot_of(member, 0)
        mirror = [posted[0, OPP[member], 2 * enter + h] * scale(2 * enter + h) for h in range(2)]

        def plane(column):
            parts = []
            for h in range(2):
                row = (8 * h + slot) * 8
                parts.append(arriving[column, row:row + 8, :])
            if cy:
                first, second = roll(parts[0], 16 * cy, 1), roll(parts[1], 16 * cy, 1)
                carried = lane < 16 if cy > 0 else lane >= 112
                parts = [jnp.where(carried, second, first), jnp.where(carried, first, second)]
            return [jnp.where(absent[column] != 0, mirror[h], parts[h]) for h in range(2)]

        def edge_plane(column):
            if cy:
                return plane(column)
            parts = []
            for h in range(2):
                row = (8 * h + slot) * 8
                parts.append(roll(arriving[column, row:row + 8, :], -15 * cz, 1))
            return [jnp.where(absent[column] != 0, mirror[h], parts[h]) for h in range(2)]

        parts = plane(toward(member, 0))
        if cz:
            column = toward(member, 0)
            parts = []
            for h in range(2):
                row = (8 * h + slot) * 8
                new = roll(arriving[column, row:row + 8, :], cz, 1)
                parts.append(jnp.where(absent[column] != 0, mirror[h], new))
        if cy or cz:
            edges = edge_plane(OPP[member] - 1)
            for h in range(2):
                if cy:
                    if side(cy)[1] // 8 != h:
                        continue
                    corner = (lane >> 4) == side(cy)[1] % 8
                else:
                    corner = (lane & 15) == side(cz)[1]
                parts[h] = jnp.where(corner, edges[h], parts[h])
        for h in range(2):
            put(member, 2 * enter + h, parts[h])


def mean_of(gathered):
    total = jnp.sum(gathered[...], axis=0, keepdims=True)
    ratio = total / pltpu.roll(total, 64, 1)
    return jnp.broadcast_to(ratio[:, 0:1], (GROUP, 128))


def collide_all(load, kinds, posted, sums, rows_out, step, bricks):
    real = iota((GROUP, 128), 0) + step * GROUP < bricks

    def chunk(c, carry):
        lanes = pl.ds(pl.multiple_of(128 * c, 128), 128)
        kind = kinds[:, lanes]
        out, density = collide([load(i, c) for i in range(19)], kind)
        for i in range(19):
            posted[0, i, c] = out[i]
        counted = real & (kind != 1)
        return (carry[0] + jnp.where(counted, density, 0.0),
                carry[1] + jnp.where(counted, 1.0, 0.0))

    zero = jnp.zeros((GROUP, 128), F32)
    total, count = lax.fori_loop(0, CHUNKS, chunk, (zero, zero))

    @pl.when(step == 0)
    def _():
        sums[0] = total
        sums[1] = count

    @pl.when(step > 0)
    def _():
        sums[0] += total
        sums[1] += count

    @pl.when(step == pl.num_programs(0) - 1)
    def _():
        left = iota(rows_out.shape, 1) < 64
        rows_out[...] = jnp.where(left, jnp.sum(sums[0]), jnp.sum(sums[1]))


def first_kernel(bricks, pops, kinds, posted, faces, marks, rows_out, layers, sums):
    step = pl.program_id(0)

    def load(i, c):
        return pops[i, :, pl.ds(pl.multiple_of(128 * c, 128), 128)]

    collide_all(load, kinds, posted, sums, rows_out, step, bricks)
    pack(lambda m, c: posted[0, m, c], layers, faces, step)

    def mark(m, c):
        lanes = pl.ds(pl.multiple_of(128 * c, 128), 128)
        return jnp.where(kinds[:, lanes] == 3, 1.0, 0.0)

    pack(mark, layers, marks, step)


def fill(pieces, table, sems):
    copies = []
    start = 0
    for k, piece in enumerate(pieces):
        count = piece.shape[0]
        copies.append(pltpu.make_async_copy(piece, table.at[pl.ds(start, count)], sems.at[k]))
        start += count
    return copies


def take_tables(refs, table, marks, sems):
    copies = fill(refs[:3], table, sems.at[0]) + fill(refs[3:], marks, sems.at[1])
    for copy in copies:
        copy.start()
    for copy in copies:
        copy.wait()


def middle_kernel(bricks, index, gathered, before, kinds, absent, own, even, odd, own_m, even_m, odd_m,
                  posted, faces, rows_out, table, marks, arriving, pops, layers, sums, sems):
    step = pl.program_id(0)

    @pl.when(step == 0)
    def _():
        take_tables((own, even, odd, own_m, even_m, odd_m), table, marks, sems)

    mean = mean_of(gathered)
    gather(index, step, table, marks, mean, arriving)

    def put(member, chunk, value):
        pops[member, chunk] = value

    stream(before, kinds, absent, arriving, mean, put)
    collide_all(lambda i, c: pops[i, c], kinds, posted, sums, rows_out, step, bricks)
    pack(lambda m, c: posted[0, m, c], layers, faces, step)


def last_kernel(index, gathered, before, kinds, absent, own, even, odd, own_m, even_m, odd_m,
                out, table, marks, arriving, sems):
    step = pl.program_id(0)

    @pl.when(step == 0)
    def _():
        take_tables((own, even, odd, own_m, even_m, odd_m), table, marks, sems)

    mean = mean_of(gathered)
    gather(index, step, table, marks, mean, arriving)

    def put(member, chunk, value):
        start = 128 * chunk
        if not isinstance(start, int):
            start = pl.multiple_of(start, 128)
        out[member, :, pl.ds(start, 128)] = value

    stream(before, kinds, absent, arriving, mean, put)


F32 = jnp.float32
BLOCK = (BRICK, 128)
POSTED = (19, CHUNKS, GROUP, 128)


def params():
    return pltpu.CompilerParams(
        dimension_semantics=("arbitrary",), vmem_limit_bytes=52 * 1024 * 1024)


def whole(*shape):
    return pl.BlockSpec(shape, lambda i: (0,) * len(shape))


SPEC_POPS = pl.BlockSpec((19, GROUP, SITES), lambda i: (0, i, 0))
SPEC_KINDS = pl.BlockSpec((GROUP, SITES), lambda i: (i, 0))
SPEC_POSTED = pl.BlockSpec((1,) + POSTED, lambda i: (i, 0, 0, 0, 0))
SPEC_ABSENT = pl.BlockSpec((18, GROUP, 128), lambda i: (0, i, 0))
SPEC_SMEM = pl.BlockSpec(memory_space=pltpu.SMEM)
SPEC_ANY = pl.BlockSpec(memory_space=pl.ANY)


def shape_of(*shape):
    return jax.ShapeDtypeStruct(shape, F32)


def first_call(pops, kinds, groups, devices):
    blocks = groups * GROUP * 6
    return pl.pallas_call(
        functools.partial(first_kernel, pops.shape[1]),
        grid=(groups,),
        in_specs=[SPEC_POPS, SPEC_KINDS],
        out_specs=[SPEC_POSTED, whole(blocks, *BLOCK), whole(blocks, *BLOCK), whole(devices, 128)],
        out_shape=[shape_of(groups, *POSTED), shape_of(blocks, *BLOCK), shape_of(blocks, *BLOCK),
                   shape_of(devices, 128)],
        scratch_shapes=[pltpu.VMEM((6, 128, 128), F32), pltpu.VMEM((2, GROUP, 128), F32)],
        compiler_params=params(),
        name="first_collide",
    )(pops, kinds)


def middle_call(bricks, index, gathered, before, kinds, absent, tables, groups, devices):
    blocks = groups * GROUP * 6
    rows = sum(t.shape[0] for t in tables[:3])
    return pl.pallas_call(
        functools.partial(middle_kernel, bricks),
        grid=(groups,),
        in_specs=[SPEC_SMEM, whole(devices, 128), SPEC_POSTED, SPEC_KINDS, SPEC_ABSENT] + [SPEC_ANY] * 6,
        out_specs=[SPEC_POSTED, whole(blocks, *BLOCK), whole(devices, 128)],
        out_shape=[shape_of(groups, *POSTED), shape_of(blocks, *BLOCK), shape_of(devices, 128)],
        scratch_shapes=[pltpu.VMEM((rows,) + BLOCK, F32), pltpu.VMEM((rows,) + BLOCK, F32),
                        pltpu.VMEM((18, 128, 128), F32), pltpu.VMEM(POSTED, F32),
                        pltpu.VMEM((6, 128, 128), F32), pltpu.VMEM((2, GROUP, 128), F32),
                        pltpu.SemaphoreType.DMA((2, 3))],
        compiler_params=params(),
        name="arrive_collide",
    )(index, gathered, before, kinds, absent, *tables)


def last_call(bricks, index, gathered, before, kinds, absent, tables, groups, devices):
    rows = sum(t.shape[0] for t in tables[:3])
    return pl.pallas_call(
        last_kernel,
        grid=(groups,),
        in_specs=[SPEC_SMEM, whole(devices, 128), SPEC_POSTED, SPEC_KINDS, SPEC_ABSENT] + [SPEC_ANY] * 6,
        out_specs=SPEC_POPS,
        out_shape=shape_of(19, bricks, SITES),
        scratch_shapes=[pltpu.VMEM((rows,) + BLOCK, F32), pltpu.VMEM((rows,) + BLOCK, F32),
                        pltpu.VMEM((18, 128, 128), F32), pltpu.SemaphoreType.DMA((2, 3))],
        compiler_params=params(),
        name="arrive_out",
    )(index, gathered, before, kinds, absent, *tables)


def share_sums(rows):
    return lax.all_to_all(rows, AXES, 0, 0, tiled=True)


def swap(layers, devices):
    even_pairs = [(i, i ^ 1) for i in range(devices)]
    odd_pairs = [(i, i + 1) for i in range(1, devices - 1, 2)]
    odd_pairs = odd_pairs + [(b, a) for a, b in odd_pairs]
    return (layers, lax.ppermute(layers, AXES, even_pairs), lax.ppermute(layers, AXES, odd_pairs))


def on_device(devices, populations, neighbours, site_flags):
    bricks = populations.shape[0]
    groups = -(-bricks // GROUP)
    padded = groups * GROUP
    blocks = padded * 6
    me = lax.axis_index(AXES)
    local = neighbours - me * bricks
    parity = me % 2
    after = jnp.where(parity == 0, blocks, 2 * blocks)
    before = jnp.where(parity == 0, 2 * blocks, blocks)
    place = jnp.where(local < 0, before + (local + bricks) * 6,
                      jnp.where(local >= bricks, after + (local - bricks) * 6, local * 6))
    index = jnp.where(neighbours < 0, 0, place + jnp.asarray(np.array(COLUMN_FACE, np.int32))[None, :])
    index = jnp.pad(index, ((0, padded - bricks), (0, 0))).reshape(-1)
    absent = jnp.pad((neighbours < 0).astype(jnp.int32), ((0, padded - bricks), (0, 0)))
    absent = jnp.broadcast_to(absent.T[:, :, None], (18, padded, 128))

    posted, faces, marks, rows = first_call(jnp.transpose(populations, (1, 0, 2)), site_flags, groups, devices)
    gathered = share_sums(rows)
    mark_tables = swap(marks, devices)
    tables = swap(faces, devices) + mark_tables
    posted, faces, rows = middle_call(
        bricks, index, gathered, posted, site_flags, absent, tables, groups, devices)
    gathered = share_sums(rows)
    tables = swap(faces, devices) + mark_tables
    out = last_call(bricks, index, gathered, posted, site_flags, absent, tables, groups, devices)
    return jnp.transpose(out, (1, 0, 2))


def solution(mesh):
    devices = mesh.shape["seg"] * mesh.shape["sub"]
    in_specs = (P(AXES, None, None), P(AXES, None), P(AXES, None))
    return jax.shard_map(
        functools.partial(on_device, devices), mesh=mesh, in_specs=in_specs,
        out_specs=P(AXES, None, None), check_vma=False)
```

```python
import functools

import jax
import jax.numpy as jnp
import numpy as np
from jax import lax
from jax.experimental import pallas as pl
from jax.experimental.pallas import tpu as pltpu
from jax.sharding import PartitionSpec as P

BRICK = 16
PLANE = 256
SITES = 4096
GROUP = 8
CHUNKS = 32
SLOTS = 32
AXES = ("seg", "sub")
INLET = 0.1

SPEEDS = [
    (0, 0, 0),
    (1, 0, 0), (-1, 0, 0), (0, 1, 0), (0, -1, 0), (0, 0, 1), (0, 0, -1),
    (1, 1, 0), (-1, -1, 0), (1, -1, 0), (-1, 1, 0),
    (1, 0, 1), (-1, 0, -1), (1, 0, -1), (-1, 0, 1),
    (0, 1, 1), (0, -1, -1), (0, 1, -1), (0, -1, 1),
]
OPP = [0, 2, 1, 4, 3, 6, 5, 8, 7, 10, 9, 12, 11, 14, 13, 16, 15, 18, 17]


def face_of(speed, dim):
    return 2 * dim + (0 if speed[dim] > 0 else 1)


MEMBERS = [[i for i in range(19) if any(face_of(SPEEDS[i], d) == f and SPEEDS[i][d] for d in range(3))]
           for f in range(6)]
COLUMN_FACE = []
for _d in range(18):
    _m = SPEEDS[OPP[_d + 1]]
    _lead = [k for k in range(3) if _m[k]][0]
    COLUMN_FACE.append(face_of(_m, _lead))


def iota(shape, dim):
    return lax.broadcasted_iota(jnp.int32, shape, dim)


def roll(x, shift, axis):
    shift = shift % x.shape[axis]
    return x if shift == 0 else pltpu.roll(x, shift, axis)


def collide(f, kind):
    fluid = kind == 0
    wall = kind == 1
    inlet = kind == 2
    outlet = kind == 3
    even = [f[2 * k + 1] + f[2 * k + 2] for k in range(9)]
    odd = [f[2 * k + 1] - f[2 * k + 2] for k in range(9)]
    density = f[0] + ((even[0] + even[1]) + (even[2] + even[3])) + (
        (even[4] + even[5]) + (even[6] + even[7])) + even[8]
    inverse = 1.0 / density
    ux = (odd[0] + odd[3] + odd[4] + odd[5] + odd[6]) * inverse
    uy = (odd[1] + odd[3] - odd[4] + odd[7] + odd[8]) * inverse
    uz = (odd[2] + odd[5] - odd[6] + odd[7] - odd[8]) * inverse
    ux = jnp.where(inlet, INLET, ux)
    uy = jnp.where(inlet, 0.0, uy)
    uz = jnp.where(inlet, 0.0, uz)
    rho = jnp.where(outlet, 1.0, density)
    base = 1.0 - 1.5 * (ux * ux + uy * uy + uz * uz)
    along = [ux, uy, uz, ux + uy, ux - uy, ux + uz, ux - uz, uy + uz, uy - uz]
    keep_even = jnp.where(fluid, -0.3, jnp.where(wall, 0.5, 0.0))
    take_even = jnp.where(fluid, 0.8, jnp.where(wall, 0.0, 0.5))
    keep_odd = jnp.where(fluid, -0.1, jnp.where(wall, -0.5, 0.0))
    take_odd = jnp.where(fluid, 0.6, jnp.where(wall, 0.0, 0.5))
    fourth = jnp.where(fluid, 0.2 / 12.0, 0.0)
    rho9 = rho * (1.0 / 9.0)
    rho18 = rho * (1.0 / 18.0)
    eq_even = []
    for k in range(9):
        scale = rho9 if k < 3 else rho18
        eq_even.append(scale * (base + 4.5 * along[k] * along[k]))
    eq_rest = (rho * (1.0 / 3.0)) * base
    g_rest = f[0] - eq_rest
    g = [even[k] - eq_even[k] for k in range(9)]
    four = 4.0 * g_rest
    gx, gy, gz = 2.0 * g[0], 2.0 * g[1], 2.0 * g[2]
    ta = four - gx - gy + (g[3] + g[4])
    tb = four - gx - gz + (g[5] + g[6])
    tc = four - gy - gz + (g[7] + g[8])
    shared = (2.0 / 7.0) * (ta + tb + tc)
    ka = (ta - shared) * fourth
    kb = (tb - shared) * fourth
    kc = (tc - shared) * fourth
    kab, kac, kbc = ka + kb, ka + kc, kb + kc
    modes = [-2.0 * kab, -2.0 * kac, -2.0 * kbc, ka, ka, kb, kb, kc, kc]
    odd9 = rho * take_odd * (1.0 / 3.0)
    odd18 = rho * take_odd * (1.0 / 6.0)
    out = [2.0 * (keep_even * f[0] + take_even * eq_rest) + 4.0 * (kab + kc)]
    for k in range(9):
        half_even = keep_even * even[k] + take_even * eq_even[k] + modes[k]
        half_odd = keep_odd * odd[k] + (odd9 if k < 3 else odd18) * along[k]
        out.append(half_even + half_odd)
        out.append(half_even - half_odd)
    return out, density


def side(heading):
    return (15, 0) if heading > 0 else (0, 15)


def slot_of(member, dim):
    return MEMBERS[face_of(SPEEDS[member], dim)].index(member)


def toward(member, dim):
    return 2 * dim + (1 if SPEEDS[member][dim] > 0 else 0)


def pack(value, layers, table, step):
    lane = iota((GROUP, 128), 1)
    for face in range(2):
        leave = 15 if face % 2 == 0 else 0
        for slot, member in enumerate(MEMBERS[face]):
            for h in range(2):
                row = (8 * h + slot) * 8
                layers[face, row:row + 8, :] = value(member, 2 * leave + h)

    def line(x, carry):
        rows = pl.ds(pl.multiple_of(8 * x, 8), 8)
        for face in range(2, 6):
            leave = 15 if face % 2 == 0 else 0
            packed = None
            for slot, member in enumerate(MEMBERS[face]):
                if face < 4:
                    piece = value(member, 2 * x + leave // 8)
                    piece = roll(piece, 16 * slot - 16 * (leave % 8), 1)
                    packed = piece if packed is None else jnp.where((lane >> 4) == slot, piece, packed)
                else:
                    for h in range(2):
                        piece = roll(value(member, 2 * x + h), 8 * h + slot - leave, 1)
                        packed = (piece if packed is None
                                  else jnp.where((lane & 15) == 8 * h + slot, piece, packed))
            layers[face, rows, :] = packed
        return carry

    lax.fori_loop(0, BRICK, line, 0)
    for face in range(6):
        for j in range(GROUP):
            table[(step * GROUP + j) * 6 + face] = layers[face, pl.ds(j, BRICK, stride=8), :]


def gather(index, step, table, marks, mean, arriving):
    wide = jnp.concatenate([mean, mean], axis=0)

    def brick(j, carry):
        base = (step * GROUP + j) * 18
        for column in range(18):
            at = index[base + column]
            block = table[at]
            arriving[column, pl.ds(j, BRICK, stride=8), :] = jnp.where(
                marks[at] != 0.0, block * wide, block)
        return carry

    lax.fori_loop(0, GROUP, brick, 0)


def stream(posted, kinds, absent, arriving, mean, put):
    lane = iota((GROUP, 128), 1)

    def scale(chunk):
        lanes = pl.ds(pl.multiple_of(128 * chunk, 128), 128)
        return jnp.where(kinds[:, lanes] == 3, mean, 1.0)

    def line(x, carry):
        before = (x + 15) & 15
        after = (x + 1) & 15
        place = {0: x, 1: before, -1: after}
        scales = {cx: (scale(2 * place[cx]), scale(2 * place[cx] + 1)) for cx in (0, 1, -1)}

        def load(member, cx, h):
            return posted[0, member, 2 * place[cx] + h] * scales[cx][h]

        for member in range(19):
            cx, cy, cz = SPEEDS[member]
            parts = [load(member, cx, h) for h in range(2)]
            mirror = [None, None]
            if cy or cz:
                mirror = [load(OPP[member], 0, h) for h in range(2)]
            if cy:
                first, second = roll(parts[0], 16 * cy, 1), roll(parts[1], 16 * cy, 1)
                carried = lane < 16 if cy > 0 else lane >= 112
                parts = [jnp.where(carried, second, first), jnp.where(carried, first, second)]
            if cz:
                parts = [roll(part, cz, 1) for part in parts]
            rows = pl.ds(pl.multiple_of(8 * place[cx], 8), 8)
            if cy:
                leave, enter = side(cy)
                column = toward(member, 1)
                half = enter // 8
                shift = 16 * (enter % 8) - 16 * slot_of(member, 1)
                here = (lane >> 4) == enter % 8
                new = roll(arriving[column, rows, :], shift + cz, 1)
                new = jnp.where(absent[column] != 0, mirror[half], new)
                parts[half] = jnp.where(here, new, parts[half])
            if cz:
                leave, enter = side(cz)
                column = toward(member, 2)
                slot = slot_of(member, 2)
                gone = absent[column] != 0
                here = (lane & 15) == enter
                block = arriving[column, rows, :]
                for h in range(2):
                    new = roll(block, 16 * cy + enter - slot - 8 * h, 1)
                    if cy and h == (1 if cy > 0 else 0):
                        other = roll(block, 16 * cy + enter - slot - 8 * (1 - h), 1)
                        new = jnp.where(lane < 16 if cy > 0 else lane >= 112, other, new)
                    new = jnp.where(gone, mirror[h], new)
                    parts[h] = jnp.where(here, new, parts[h])
            if cy and cz:
                leave, enter = side(cy)
                column = OPP[member] - 1
                half = enter // 8
                shift = 16 * (enter % 8) - 16 * slot_of(member, 1)
                corner = ((lane >> 4) == enter % 8) & ((lane & 15) == side(cz)[1])
                new = roll(arriving[column, rows, :], shift - 15 * cz, 1)
                new = jnp.where(absent[column] != 0, mirror[half], new)
                parts[half] = jnp.where(corner, new, parts[half])
            for h in range(2):
                put(member, 2 * x + h, parts[h])
        return carry

    lax.fori_loop(0, BRICK, line, 0)

    for member in range(19):
        cx, cy, cz = SPEEDS[member]
        if not cx:
            continue
        leave, enter = side(cx)
        slot = slot_of(member, 0)
        mirror = [posted[0, OPP[member], 2 * enter + h] * scale(2 * enter + h) for h in range(2)]

        def plane(column):
            parts = []
            for h in range(2):
                row = (8 * h + slot) * 8
                parts.append(arriving[column, row:row + 8, :])
            if cy:
                first, second = roll(parts[0], 16 * cy, 1), roll(parts[1], 16 * cy, 1)
                carried = lane < 16 if cy > 0 else lane >= 112
                parts = [jnp.where(carried, second, first), jnp.where(carried, first, second)]
            return [jnp.where(absent[column] != 0, mirror[h], parts[h]) for h in range(2)]

        def edge_plane(column):
            if cy:
                return plane(column)
            parts = []
            for h in range(2):
                row = (8 * h + slot) * 8
                parts.append(roll(arriving[column, row:row + 8, :], -15 * cz, 1))
            return [jnp.where(absent[column] != 0, mirror[h], parts[h]) for h in range(2)]

        parts = plane(toward(member, 0))
        if cz:
            column = toward(member, 0)
            parts = []
            for h in range(2):
                row = (8 * h + slot) * 8
                new = roll(arriving[column, row:row + 8, :], cz, 1)
                parts.append(jnp.where(absent[column] != 0, mirror[h], new))
        if cy or cz:
            edges = edge_plane(OPP[member] - 1)
            for h in range(2):
                if cy:
                    if side(cy)[1] // 8 != h:
                        continue
                    corner = (lane >> 4) == side(cy)[1] % 8
                else:
                    corner = (lane & 15) == side(cz)[1]
                parts[h] = jnp.where(corner, edges[h], parts[h])
        for h in range(2):
            put(member, 2 * enter + h, parts[h])


def mean_of(gathered):
    total = jnp.sum(gathered[...], axis=0, keepdims=True)
    ratio = total / pltpu.roll(total, 64, 1)
    return jnp.broadcast_to(ratio[:, 0:1], (GROUP, 128))


def collide_all(load, kinds, posted, sums, rows_out, step, bricks, excess):
    real = iota((GROUP, 128), 0) + step * GROUP < bricks

    def chunk(c, carry):
        lanes = pl.ds(pl.multiple_of(128 * c, 128), 128)
        kind = kinds[:, lanes]
        out, density = collide([load(i, c) for i in range(19)], kind)
        for i in range(19):
            posted[0, i, c] = out[i]
        counted = real & (kind != 1)
        return (carry[0] + jnp.where(counted, density, 0.0),
                carry[1] + jnp.where(counted, 1.0, 0.0))

    zero = jnp.zeros((GROUP, 128), F32)
    total, count = lax.fori_loop(0, CHUNKS, chunk, (zero, zero))

    @pl.when(step == 0)
    def _():
        sums[0] = total
        sums[1] = count

    @pl.when(step > 0)
    def _():
        sums[0] += total
        sums[1] += count

    @pl.when(step == pl.num_programs(0) - 1)
    def _():
        lane = iota(rows_out.shape, 1)
        both = jnp.where(lane < 64, jnp.sum(sums[0]), jnp.sum(sums[1]))
        rows_out[...] = jnp.where(lane == 127, excess, both)


def select_blocks(lists, table, send, start):
    slots = lists.shape[0] // 2 - 1

    @pl.when(pl.program_id(0) == pl.num_programs(0) - 1)
    def _():
        def slot(s, carry):
            for partner in range(2):
                send[partner, start + s] = table[lists[partner * (slots + 1) + s]]
            return carry

        lax.fori_loop(0, slots, slot, 0)


def first_kernel(bricks, lists, pops, kinds, posted, faces, marks, send, rows_out, layers, sums):
    step = pl.program_id(0)
    slots = lists.shape[0] // 2 - 1
    excess = (lists[slots] + lists[2 * slots + 1]).astype(F32)

    def load(i, c):
        return pops[i, :, pl.ds(pl.multiple_of(128 * c, 128), 128)]

    collide_all(load, kinds, posted, sums, rows_out, step, bricks, excess)
    pack(lambda m, c: posted[0, m, c], layers, faces, step)

    def mark(m, c):
        lanes = pl.ds(pl.multiple_of(128 * c, 128), 128)
        return jnp.where(kinds[:, lanes] == 3, 1.0, 0.0)

    pack(mark, layers, marks, step)
    select_blocks(lists, faces, send, 0)
    select_blocks(lists, marks, send, slots)


def take_tables(slots, own, own_marks, sent, sent_before, table, marks, sems):
    blocks = own.shape[0]
    copies = [pltpu.make_async_copy(own, table.at[pl.ds(0, blocks)], sems.at[0]),
              pltpu.make_async_copy(own_marks, marks.at[pl.ds(0, blocks)], sems.at[1])]
    for partner in range(2):
        rows = pl.ds(blocks + partner * slots, slots)
        copies.append(pltpu.make_async_copy(
            sent[partner].at[pl.ds(0, slots)], table.at[rows], sems.at[2 + partner]))
        copies.append(pltpu.make_async_copy(
            sent_before[partner].at[pl.ds(slots, slots)], marks.at[rows], sems.at[4 + partner]))
    for copy in copies:
        copy.start()
    for copy in copies:
        copy.wait()


def middle_kernel(bricks, lists, index, gathered, before, kinds, absent, own, own_m, even, odd,
                  posted, faces, send, rows_out, table, marks, arriving, pops, layers, sums, sems):
    step = pl.program_id(0)
    slots = lists.shape[0] // 2 - 1

    @pl.when(step == 0)
    def _():
        take_tables(slots, own, own_m, (even, odd), (even, odd), table, marks, sems)

    mean = mean_of(gathered)
    gather(index, step, table, marks, mean, arriving)

    def put(member, chunk, value):
        pops[member, chunk] = value

    stream(before, kinds, absent, arriving, mean, put)
    collide_all(lambda i, c: pops[i, c], kinds, posted, sums, rows_out, step, bricks, 0.0)
    pack(lambda m, c: posted[0, m, c], layers, faces, step)
    select_blocks(lists, faces, send, 0)


def last_kernel(slots, index, gathered, before, kinds, absent, own, own_m, even, odd, even_1, odd_1,
                out, table, marks, arriving, sems):
    step = pl.program_id(0)

    @pl.when(step == 0)
    def _():
        take_tables(slots, own, own_m, (even, odd), (even_1, odd_1), table, marks, sems)

    mean = mean_of(gathered)
    gather(index, step, table, marks, mean, arriving)

    def put(member, chunk, value):
        start = 128 * chunk
        if not isinstance(start, int):
            start = pl.multiple_of(start, 128)
        out[member, :, pl.ds(start, 128)] = value

    stream(before, kinds, absent, arriving, mean, put)


F32 = jnp.float32
BLOCK = (BRICK, 128)
POSTED = (19, CHUNKS, GROUP, 128)


def params():
    return pltpu.CompilerParams(
        dimension_semantics=("arbitrary",), vmem_limit_bytes=52 * 1024 * 1024)


def whole(*shape):
    return pl.BlockSpec(shape, lambda i: (0,) * len(shape))


SPEC_POPS = pl.BlockSpec((19, GROUP, SITES), lambda i: (0, i, 0))
SPEC_KINDS = pl.BlockSpec((GROUP, SITES), lambda i: (i, 0))
SPEC_POSTED = pl.BlockSpec((1,) + POSTED, lambda i: (i, 0, 0, 0, 0))
SPEC_ABSENT = pl.BlockSpec((18, GROUP, 128), lambda i: (0, i, 0))
SPEC_SMEM = pl.BlockSpec(memory_space=pltpu.SMEM)
SPEC_ANY = pl.BlockSpec(memory_space=pl.ANY)


def shape_of(*shape):
    return jax.ShapeDtypeStruct(shape, F32)


def first_call(lists, pops, kinds, groups, devices):
    blocks = groups * GROUP * 6
    slots = lists.shape[0] // 2 - 1
    return pl.pallas_call(
        functools.partial(first_kernel, pops.shape[1]),
        grid=(groups,),
        in_specs=[SPEC_SMEM, SPEC_POPS, SPEC_KINDS],
        out_specs=[SPEC_POSTED, whole(blocks, *BLOCK), whole(blocks, *BLOCK),
                   whole(2, 2 * slots, *BLOCK), whole(devices, 128)],
        out_shape=[shape_of(groups, *POSTED), shape_of(blocks, *BLOCK), shape_of(blocks, *BLOCK),
                   shape_of(2, 2 * slots, *BLOCK), shape_of(devices, 128)],
        scratch_shapes=[pltpu.VMEM((6, 128, 128), F32), pltpu.VMEM((2, GROUP, 128), F32)],
        compiler_params=params(),
        name="first_collide",
    )(lists, pops, kinds)


def middle_call(bricks, lists, index, gathered, before, kinds, absent, tables, groups, devices):
    blocks = groups * GROUP * 6
    slots = lists.shape[0] // 2 - 1
    rows = blocks + 2 * slots
    return pl.pallas_call(
        functools.partial(middle_kernel, bricks),
        grid=(groups,),
        in_specs=[SPEC_SMEM, SPEC_SMEM, whole(devices, 128), SPEC_POSTED, SPEC_KINDS,
                  SPEC_ABSENT] + [SPEC_ANY] * 4,
        out_specs=[SPEC_POSTED, whole(blocks, *BLOCK), whole(2, slots, *BLOCK), whole(devices, 128)],
        out_shape=[shape_of(groups, *POSTED), shape_of(blocks, *BLOCK), shape_of(2, slots, *BLOCK),
                   shape_of(devices, 128)],
        scratch_shapes=[pltpu.VMEM((rows,) + BLOCK, F32), pltpu.VMEM((rows,) + BLOCK, F32),
                        pltpu.VMEM((18, 128, 128), F32), pltpu.VMEM(POSTED, F32),
                        pltpu.VMEM((6, 128, 128), F32), pltpu.VMEM((2, GROUP, 128), F32),
                        pltpu.SemaphoreType.DMA((6,))],
        compiler_params=params(),
        name="arrive_collide",
    )(lists, index, gathered, before, kinds, absent, *tables)


def last_call(bricks, slots, index, gathered, before, kinds, absent, tables, groups, devices):
    rows = groups * GROUP * 6 + 2 * slots
    return pl.pallas_call(
        functools.partial(last_kernel, slots),
        grid=(groups,),
        in_specs=[SPEC_SMEM, whole(devices, 128), SPEC_POSTED, SPEC_KINDS, SPEC_ABSENT] + [SPEC_ANY] * 6,
        out_specs=SPEC_POPS,
        out_shape=shape_of(19, bricks, SITES),
        scratch_shapes=[pltpu.VMEM((rows,) + BLOCK, F32), pltpu.VMEM((rows,) + BLOCK, F32),
                        pltpu.VMEM((18, 128, 128), F32), pltpu.SemaphoreType.DMA((6,))],
        compiler_params=params(),
        name="arrive_out",
    )(index, gathered, before, kinds, absent, *tables)


def share_sums(rows):
    return lax.all_to_all(rows, AXES, 0, 0, tiled=True)


def swap(send, devices):
    even_pairs = [(i, i ^ 1) for i in range(devices)]
    odd_pairs = [(i, i + 1) for i in range(1, devices - 1, 2)]
    odd_pairs = odd_pairs + [(b, a) for a, b in odd_pairs]
    return lax.ppermute(send[0], AXES, even_pairs), lax.ppermute(send[1], AXES, odd_pairs)


def rank(used):
    count = used.shape[0]
    return jnp.sum(jnp.where(iota((count, count), 1) < iota((count, count), 0), used[None, :], 0), axis=1)


def exchange_plan(neighbours, slots, padded):
    bricks = neighbours.shape[0]
    blocks = bricks * 6
    me = lax.axis_index(AXES)
    local = neighbours - me * bricks
    present = neighbours >= 0
    following = present & (local >= bricks)
    preceding = present & (local < 0)
    first = me % 2 == 0
    read = jnp.asarray(np.array(COLUMN_FACE, np.int32))
    given = jnp.asarray(np.array([COLUMN_FACE[OPP[d + 1] - 1] for d in range(18)], np.int32))
    faces = jnp.arange(6, dtype=jnp.int32)
    index = local * 6 + read[None, :]
    lists = []
    for partner in range(2):
        is_next = first if partner == 0 else ~first
        there = jnp.where(is_next, following, preceding)
        spot = (local + jnp.where(is_next, -bricks, bricks)) * 6 + read[None, :]
        used = jnp.any(there[:, :, None] & (given[:, None] == faces[None, :])[None], axis=1)
        used = used.astype(jnp.int32).reshape(-1)
        order = jnp.where(used == 1, rank(used), blocks)
        chosen = order[None, :] == iota((slots, blocks), 0)
        lists.append(jnp.sum(jnp.where(chosen, iota((slots, blocks), 1), 0), axis=1))
        lists.append(jnp.where(jnp.sum(used) > slots, 1, 0)[None])
        flat = jnp.where(there, spot, -1).reshape(-1)
        hits = flat[:, None] == iota((flat.shape[0], blocks), 1)
        ranks = rank(jnp.any(hits, axis=0).astype(jnp.int32))
        at = jnp.sum(jnp.where(hits, jnp.minimum(ranks, slots - 1)[None, :], 0), axis=1)
        index = jnp.where(there, padded * 6 + partner * slots + at.reshape(bricks, 18), index)
    index = jnp.where(present, index, 0)
    index = jnp.pad(index, ((0, padded - bricks), (0, 0))).reshape(-1)
    return jnp.concatenate(lists), index


def begin(devices, slots, populations, neighbours, site_flags, absent):
    bricks = populations.shape[1]
    groups = absent.shape[1] // GROUP
    lists, index = exchange_plan(neighbours, slots, groups * GROUP)
    posted, faces, marks, send, rows = first_call(lists, populations, site_flags, groups, devices)
    gathered = share_sums(rows)
    sent_first = swap(send, devices)
    excess = jnp.sum(gathered[:, 127])
    posted, faces, send, rows = middle_call(
        bricks, lists, index, gathered, posted, site_flags, absent,
        (faces, marks) + sent_first, groups, devices)
    gathered = share_sums(rows)
    sent = swap(send, devices)
    return excess, (index, gathered, posted, faces, marks) + sent + sent_first


def finish(devices, slots, site_flags, absent, bricks, state):
    index, gathered, posted, faces, marks = state[:5]
    return last_call(bricks, slots, index, gathered, posted, site_flags, absent,
                     (faces, marks) + state[5:], absent.shape[1] // GROUP, devices)


def on_device(devices, populations, neighbours, site_flags):
    bricks = populations.shape[0]
    padded = -(-bricks // GROUP) * GROUP
    absent = jnp.pad((neighbours < 0).astype(jnp.int32), ((0, padded - bricks), (0, 0)))
    absent = jnp.broadcast_to(absent.T[:, :, None], (18, padded, 128))
    populations = jnp.transpose(populations, (1, 0, 2))
    excess, state = begin(devices, SLOTS, populations, neighbours, site_flags, absent)

    def enough(populations, neighbours, state):
        return finish(devices, SLOTS, site_flags, absent, bricks, state)

    def too_few(populations, neighbours, state):
        every = bricks * 6
        _, state = begin(devices, every, populations, neighbours, site_flags, absent)
        return finish(devices, every, site_flags, absent, bricks, state)

    out = lax.cond(excess > 0.0, too_few, enough, populations, neighbours, state)
    return jnp.transpose(out, (1, 0, 2))


def solution(mesh):
    devices = mesh.shape["seg"] * mesh.shape["sub"]
    in_specs = (P(AXES, None, None), P(AXES, None), P(AXES, None))
    return jax.shard_map(
        functools.partial(on_device, devices), mesh=mesh, in_specs=in_specs,
        out_specs=P(AXES, None, None), check_vma=False)
```

```python
import functools

import jax
import jax.numpy as jnp
import numpy as np
from jax import lax
from jax.experimental import pallas as pl
from jax.experimental.pallas import tpu as pltpu
from jax.sharding import PartitionSpec as P

BRICK = 16
PLANE = 256
SITES = 4096
GROUP = 8
CHUNKS = 32
LIMIT = 52
SLOTS = 32
AXES = ("seg", "sub")
INLET = 0.1

SPEEDS = [
    (0, 0, 0),
    (1, 0, 0), (-1, 0, 0), (0, 1, 0), (0, -1, 0), (0, 0, 1), (0, 0, -1),
    (1, 1, 0), (-1, -1, 0), (1, -1, 0), (-1, 1, 0),
    (1, 0, 1), (-1, 0, -1), (1, 0, -1), (-1, 0, 1),
    (0, 1, 1), (0, -1, -1), (0, 1, -1), (0, -1, 1),
]
OPP = [0, 2, 1, 4, 3, 6, 5, 8, 7, 10, 9, 12, 11, 14, 13, 16, 15, 18, 17]


def face_of(speed, dim):
    return 2 * dim + (0 if speed[dim] > 0 else 1)


MEMBERS = [[i for i in range(19) if any(face_of(SPEEDS[i], d) == f and SPEEDS[i][d] for d in range(3))]
           for f in range(6)]
COLUMN_FACE = []
for _d in range(18):
    _m = SPEEDS[OPP[_d + 1]]
    _lead = [k for k in range(3) if _m[k]][0]
    COLUMN_FACE.append(face_of(_m, _lead))


def iota(shape, dim):
    return lax.broadcasted_iota(jnp.int32, shape, dim)


def roll(x, shift, axis):
    shift = shift % x.shape[axis]
    return x if shift == 0 else pltpu.roll(x, shift, axis)


def collide(f, kind):
    fluid = kind == 0
    wall = kind == 1
    inlet = kind == 2
    outlet = kind == 3
    even = [f[2 * k + 1] + f[2 * k + 2] for k in range(9)]
    odd = [f[2 * k + 1] - f[2 * k + 2] for k in range(9)]
    density = f[0] + ((even[0] + even[1]) + (even[2] + even[3])) + (
        (even[4] + even[5]) + (even[6] + even[7])) + even[8]
    inverse = 1.0 / density
    ux = (odd[0] + odd[3] + odd[4] + odd[5] + odd[6]) * inverse
    uy = (odd[1] + odd[3] - odd[4] + odd[7] + odd[8]) * inverse
    uz = (odd[2] + odd[5] - odd[6] + odd[7] - odd[8]) * inverse
    ux = jnp.where(inlet, INLET, ux)
    uy = jnp.where(inlet, 0.0, uy)
    uz = jnp.where(inlet, 0.0, uz)
    rho = jnp.where(outlet, 1.0, density)
    base = 1.0 - 1.5 * (ux * ux + uy * uy + uz * uz)
    along = [ux, uy, uz, ux + uy, ux - uy, ux + uz, ux - uz, uy + uz, uy - uz]
    keep_even = jnp.where(fluid, -0.3, jnp.where(wall, 0.5, 0.0))
    take_even = jnp.where(fluid, 0.8, jnp.where(wall, 0.0, 0.5))
    keep_odd = jnp.where(fluid, -0.1, jnp.where(wall, -0.5, 0.0))
    take_odd = jnp.where(fluid, 0.6, jnp.where(wall, 0.0, 0.5))
    fourth = jnp.where(fluid, 0.2 / 12.0, 0.0)
    rho9 = rho * (1.0 / 9.0)
    rho18 = rho * (1.0 / 18.0)
    eq_even = []
    for k in range(9):
        scale = rho9 if k < 3 else rho18
        eq_even.append(scale * (base + 4.5 * along[k] * along[k]))
    eq_rest = (rho * (1.0 / 3.0)) * base
    g_rest = f[0] - eq_rest
    g = [even[k] - eq_even[k] for k in range(9)]
    four = 4.0 * g_rest
    gx, gy, gz = 2.0 * g[0], 2.0 * g[1], 2.0 * g[2]
    ta = four - gx - gy + (g[3] + g[4])
    tb = four - gx - gz + (g[5] + g[6])
    tc = four - gy - gz + (g[7] + g[8])
    shared = (2.0 / 7.0) * (ta + tb + tc)
    ka = (ta - shared) * fourth
    kb = (tb - shared) * fourth
    kc = (tc - shared) * fourth
    kab, kac, kbc = ka + kb, ka + kc, kb + kc
    modes = [-2.0 * kab, -2.0 * kac, -2.0 * kbc, ka, ka, kb, kb, kc, kc]
    odd9 = rho * take_odd * (1.0 / 3.0)
    odd18 = rho * take_odd * (1.0 / 6.0)
    out = [2.0 * (keep_even * f[0] + take_even * eq_rest) + 4.0 * (kab + kc)]
    for k in range(9):
        half_even = keep_even * even[k] + take_even * eq_even[k] + modes[k]
        half_odd = keep_odd * odd[k] + (odd9 if k < 3 else odd18) * along[k]
        out.append(half_even + half_odd)
        out.append(half_even - half_odd)
    return out, density


def side(heading):
    return (15, 0) if heading > 0 else (0, 15)


def slot_of(member, dim):
    return MEMBERS[face_of(SPEEDS[member], dim)].index(member)


def toward(member, dim):
    return 2 * dim + (1 if SPEEDS[member][dim] > 0 else 0)


def pack(value, mark, layers, table, step):
    lane = iota((GROUP, 128), 1)
    for face in range(2):
        leave = 15 if face % 2 == 0 else 0
        for slot, member in enumerate(MEMBERS[face]):
            for h in range(2):
                row = (8 * h + slot) * 8
                layers[face, row:row + 8, :] = value(member, 2 * leave + h)
        for h in range(2):
            row = (8 * h + 5) * 8
            layers[face, row:row + 8, :] = mark(2 * leave + h)

    def line(x, carry):
        rows = pl.ds(pl.multiple_of(8 * x, 8), 8)
        outlet = [mark(2 * x + h) for h in range(2)]
        for face in range(2, 6):
            leave = 15 if face % 2 == 0 else 0
            packed = None
            for slot, member in enumerate(MEMBERS[face] + [None]):
                if face < 4:
                    piece = outlet[leave // 8] if member is None else value(member, 2 * x + leave // 8)
                    piece = roll(piece, 16 * slot - 16 * (leave % 8), 1)
                    packed = piece if packed is None else jnp.where((lane >> 4) == slot, piece, packed)
                else:
                    for h in range(2):
                        piece = outlet[h] if member is None else value(member, 2 * x + h)
                        piece = roll(piece, 8 * h + slot - leave, 1)
                        packed = (piece if packed is None
                                  else jnp.where((lane & 15) == 8 * h + slot, piece, packed))
            layers[face, rows, :] = packed
        return carry

    lax.fori_loop(0, BRICK, line, 0, unroll=4)
    unpack(layers, table, step)


def unpack(layers, table, step):
    for face in range(6):
        for j in range(GROUP):
            table[(step * GROUP + j) * 6 + face] = layers[face, pl.ds(j, BRICK, stride=8), :]


def scaled(block, face, mean):
    if face < 2:
        parts = []
        for h in range(2):
            part = block[8 * h:8 * h + 8, :]
            parts.append(jnp.where(jnp.broadcast_to(part[5:6, :], (8, 128)) != 0.0, part * mean, part))
        return jnp.concatenate(parts, axis=0)
    lane = iota(BLOCK, 1)
    by = 16 if face < 4 else 1
    slot = jnp.minimum(lane >> 4, 5) if face < 4 else jnp.minimum(lane & 7, 5)
    marks = jnp.take_along_axis(block, lane + (5 - slot) * by, axis=1, mode="promise_in_bounds")
    return jnp.where((slot < 5) & (marks != 0.0), block * jnp.concatenate([mean, mean], axis=0), block)


def gather(bricks, index, step, table, mean, arriving):
    def brick(j, carry):
        base = (step * GROUP + j) * 18
        for column in range(18):
            block = scaled(table[index[base + column]], COLUMN_FACE[column], mean)
            arriving[column, pl.ds(j, BRICK, stride=8), :] = block
        return carry

    lax.fori_loop(0, jnp.minimum(GROUP, bricks - step * GROUP), brick, 0)


def stream(posted, kinds, absent, arriving, mean, put):
    lane = iota((GROUP, 128), 1)

    def scale(chunk):
        lanes = pl.ds(pl.multiple_of(128 * chunk, 128), 128)
        return jnp.where(kinds[:, lanes] == 3, mean, 1.0)

    def line(x, carry):
        before = (x + 15) & 15
        after = (x + 1) & 15
        place = {0: x, 1: before, -1: after}
        scales = {cx: (scale(2 * place[cx]), scale(2 * place[cx] + 1)) for cx in (0, 1, -1)}

        for member in range(19):
            if member % 2 == 1 or member == 0:
                loaded = {}

            def load(member, cx, h):
                if (member, cx, h) not in loaded:
                    loaded[member, cx, h] = posted[0, member, 2 * place[cx] + h] * scales[cx][h]
                return loaded[member, cx, h]

            cx, cy, cz = SPEEDS[member]
            parts = [load(member, cx, h) for h in range(2)]
            mirror = [None, None]
            if cy or cz:
                mirror = [load(OPP[member], 0, h) for h in range(2)]
            if cy:
                by = 16 * cy + cz
                first, second = roll(parts[0], by, 1), roll(parts[1], by, 1)
                carried = lane < by if cy > 0 else lane >= 128 + by
                parts = [jnp.where(carried, second, first), jnp.where(carried, first, second)]
            elif cz:
                parts = [roll(part, cz, 1) for part in parts]
            rows = pl.ds(pl.multiple_of(8 * place[cx], 8), 8)
            if cy:
                leave, enter = side(cy)
                column = toward(member, 1)
                half = enter // 8
                shift = 16 * (enter % 8) - 16 * slot_of(member, 1)
                here = (lane >> 4) == enter % 8
                new = roll(arriving[column, rows, :], shift + cz, 1)
                new = jnp.where(absent[column] != 0, mirror[half], new)
                parts[half] = jnp.where(here, new, parts[half])
            if cz:
                leave, enter = side(cz)
                column = toward(member, 2)
                slot = slot_of(member, 2)
                gone = absent[column] != 0
                here = (lane & 15) == enter
                block = arriving[column, rows, :]
                for h in range(2):
                    new = roll(block, 16 * cy + enter - slot - 8 * h, 1)
                    if cy and h == (1 if cy > 0 else 0):
                        other = roll(block, 16 * cy + enter - slot - 8 * (1 - h), 1)
                        new = jnp.where(lane < 16 if cy > 0 else lane >= 112, other, new)
                    new = jnp.where(gone, mirror[h], new)
                    parts[h] = jnp.where(here, new, parts[h])
            if cy and cz:
                leave, enter = side(cy)
                column = OPP[member] - 1
                half = enter // 8
                shift = 16 * (enter % 8) - 16 * slot_of(member, 1)
                corner = ((lane >> 4) == enter % 8) & ((lane & 15) == side(cz)[1])
                new = roll(arriving[column, rows, :], shift - 15 * cz, 1)
                new = jnp.where(absent[column] != 0, mirror[half], new)
                parts[half] = jnp.where(corner, new, parts[half])
            for h in range(2):
                put(member, 2 * x + h, parts[h])
        return carry

    lax.fori_loop(0, BRICK, line, 0, unroll=2)

    for member in range(19):
        cx, cy, cz = SPEEDS[member]
        if not cx:
            continue
        leave, enter = side(cx)
        slot = slot_of(member, 0)
        mirror = [posted[0, OPP[member], 2 * enter + h] * scale(2 * enter + h) for h in range(2)]

        def plane(column):
            parts = []
            for h in range(2):
                row = (8 * h + slot) * 8
                parts.append(arriving[column, row:row + 8, :])
            if cy:
                first, second = roll(parts[0], 16 * cy, 1), roll(parts[1], 16 * cy, 1)
                carried = lane < 16 if cy > 0 else lane >= 112
                parts = [jnp.where(carried, second, first), jnp.where(carried, first, second)]
            return [jnp.where(absent[column] != 0, mirror[h], parts[h]) for h in range(2)]

        def edge_plane(column):
            if cy:
                return plane(column)
            parts = []
            for h in range(2):
                row = (8 * h + slot) * 8
                parts.append(roll(arriving[column, row:row + 8, :], -15 * cz, 1))
            return [jnp.where(absent[column] != 0, mirror[h], parts[h]) for h in range(2)]

        parts = plane(toward(member, 0))
        if cz:
            column = toward(member, 0)
            parts = []
            for h in range(2):
                row = (8 * h + slot) * 8
                new = roll(arriving[column, row:row + 8, :], cz, 1)
                parts.append(jnp.where(absent[column] != 0, mirror[h], new))
        if cy or cz:
            edges = edge_plane(OPP[member] - 1)
            for h in range(2):
                if cy:
                    if side(cy)[1] // 8 != h:
                        continue
                    corner = (lane >> 4) == side(cy)[1] % 8
                else:
                    corner = (lane & 15) == side(cz)[1]
                parts[h] = jnp.where(corner, edges[h], parts[h])
        for h in range(2):
            put(member, 2 * enter + h, parts[h])


def mean_of(gathered):
    total = jnp.sum(gathered[...], axis=0, keepdims=True)
    ratio = total / pltpu.roll(total, 64, 1)
    return jnp.broadcast_to(ratio[:, 0:1], (GROUP, 128))


def collide_all(load, kinds, posted, sums, rows_out, step, bricks, excess):
    real = iota((GROUP, 128), 0) + step * GROUP < bricks

    def chunk(c, carry):
        lanes = pl.ds(pl.multiple_of(128 * c, 128), 128)
        kind = kinds[:, lanes]
        out, density = collide([load(i, c) for i in range(19)], kind)
        for i in range(19):
            posted[0, i, c] = out[i]
        counted = real & (kind != 1)
        return (carry[0] + jnp.where(counted, density, 0.0),
                carry[1] + jnp.where(counted, 1.0, 0.0))

    zero = jnp.zeros((GROUP, 128), F32)
    total, count = lax.fori_loop(0, CHUNKS, chunk, (zero, zero), unroll=4)

    @pl.when(step == 0)
    def _():
        sums[0] = total
        sums[1] = count

    @pl.when(step > 0)
    def _():
        sums[0] += total
        sums[1] += count

    @pl.when(step == pl.num_programs(0) - 1)
    def _():
        lane = iota(rows_out.shape, 1)
        both = jnp.where(lane < 64, jnp.sum(sums[0]), jnp.sum(sums[1]))
        rows_out[...] = jnp.where(lane == 127, excess, both)


def select_blocks(lists, table, send):
    slots = lists.shape[0] // 2 - 1

    @pl.when(pl.program_id(0) == pl.num_programs(0) - 1)
    def _():
        def slot(s, carry):
            for partner in range(2):
                send[partner][s] = table[lists[partner * (slots + 1) + s]]
            return carry

        lax.fori_loop(0, slots, slot, 0, unroll=4)


def outlet_mark(kinds):
    def mark(chunk):
        start = 128 * chunk
        if not isinstance(start, int):
            start = pl.multiple_of(start, 128)
        return jnp.where(kinds[:, pl.ds(start, 128)] == 3, 1.0, 0.0)

    return mark


def first_kernel(bricks, lists, pops, kinds, posted, faces, send_even, send_odd, rows_out, layers, sums):
    step = pl.program_id(0)
    slots = lists.shape[0] // 2 - 1
    excess = (lists[slots] + lists[2 * slots + 1]).astype(F32)

    def load(i, c):
        return pops[i, :, pl.ds(pl.multiple_of(128 * c, 128), 128)]

    collide_all(load, kinds, posted, sums, rows_out, step, bricks, excess)
    pack(lambda m, c: posted[0, m, c], outlet_mark(kinds), layers, faces, step)
    select_blocks(lists, faces, (send_even, send_odd))


def take_table(pieces, table, sems):
    copies = []
    start = 0
    for k, piece in enumerate(pieces):
        count = piece.shape[0]
        copies.append(pltpu.make_async_copy(piece, table.at[pl.ds(start, count)], sems.at[k]))
        start += count
    for copy in copies:
        copy.start()
    for copy in copies:
        copy.wait()


def middle_kernel(bricks, lists, index, gathered, before, kinds, absent, own, even, odd,
                  posted, faces, send_even, send_odd, rows_out, table, arriving, pops, layers, sums, sems):
    step = pl.program_id(0)

    @pl.when(step == 0)
    def _():
        take_table((own, even, odd), table, sems)

    mean = mean_of(gathered)
    gather(bricks, index, step, table, mean, arriving)

    def put(member, chunk, value):
        pops[member, chunk] = value

    stream(before, kinds, absent, arriving, mean, put)
    collide_all(lambda i, c: pops[i, c], kinds, posted, sums, rows_out, step, bricks, 0.0)
    pack(lambda m, c: posted[0, m, c], outlet_mark(kinds), layers, faces, step)
    select_blocks(lists, faces, (send_even, send_odd))


def last_kernel(bricks, index, gathered, before, kinds, absent, own, even, odd, out, table, arriving, sems):
    step = pl.program_id(0)

    @pl.when(step == 0)
    def _():
        take_table((own, even, odd), table, sems)

    mean = mean_of(gathered)
    gather(bricks, index, step, table, mean, arriving)

    def put(member, chunk, value):
        start = 128 * chunk
        if not isinstance(start, int):
            start = pl.multiple_of(start, 128)
        out[member, :, pl.ds(start, 128)] = value

    stream(before, kinds, absent, arriving, mean, put)


F32 = jnp.float32
BLOCK = (BRICK, 128)
POSTED = (19, CHUNKS, GROUP, 128)


def params():
    return pltpu.CompilerParams(
        dimension_semantics=("arbitrary",), vmem_limit_bytes=LIMIT * 1024 * 1024)


def whole(*shape):
    return pl.BlockSpec(shape, lambda i: (0,) * len(shape))


SPEC_POPS = pl.BlockSpec((19, GROUP, SITES), lambda i: (0, i, 0))
SPEC_KINDS = pl.BlockSpec((GROUP, SITES), lambda i: (i, 0))
SPEC_POSTED = pl.BlockSpec((1,) + POSTED, lambda i: (i, 0, 0, 0, 0))
SPEC_ABSENT = pl.BlockSpec((18, GROUP, 128), lambda i: (0, i, 0))
SPEC_SMEM = pl.BlockSpec(memory_space=pltpu.SMEM)
SPEC_ANY = pl.BlockSpec(memory_space=pl.ANY)


def shape_of(*shape):
    return jax.ShapeDtypeStruct(shape, F32)


def first_call(lists, pops, kinds, groups, devices):
    blocks = groups * GROUP * 6
    slots = lists.shape[0] // 2 - 1
    return pl.pallas_call(
        functools.partial(first_kernel, pops.shape[1]),
        grid=(groups,),
        in_specs=[SPEC_SMEM, SPEC_POPS, SPEC_KINDS],
        out_specs=[SPEC_POSTED, whole(blocks, *BLOCK), whole(slots, *BLOCK), whole(slots, *BLOCK),
                   whole(devices, 128)],
        out_shape=[shape_of(groups, *POSTED), shape_of(blocks, *BLOCK), shape_of(slots, *BLOCK),
                   shape_of(slots, *BLOCK), shape_of(devices, 128)],
        scratch_shapes=[pltpu.VMEM((6, 128, 128), F32), pltpu.VMEM((2, GROUP, 128), F32)],
        compiler_params=params(),
        name="first_collide",
    )(lists, pops, kinds)


def middle_call(bricks, lists, index, gathered, before, kinds, absent, tables, groups, devices):
    blocks = groups * GROUP * 6
    slots = lists.shape[0] // 2 - 1
    return pl.pallas_call(
        functools.partial(middle_kernel, bricks),
        grid=(groups,),
        in_specs=[SPEC_SMEM, SPEC_SMEM, whole(devices, 128), SPEC_POSTED, SPEC_KINDS,
                  SPEC_ABSENT] + [SPEC_ANY] * 3,
        out_specs=[SPEC_POSTED, whole(blocks, *BLOCK), whole(slots, *BLOCK), whole(slots, *BLOCK),
                   whole(devices, 128)],
        out_shape=[shape_of(groups, *POSTED), shape_of(blocks, *BLOCK), shape_of(slots, *BLOCK),
                   shape_of(slots, *BLOCK), shape_of(devices, 128)],
        scratch_shapes=[pltpu.VMEM((blocks + 2 * slots,) + BLOCK, F32),
                        pltpu.VMEM((18, 128, 128), F32), pltpu.VMEM(POSTED, F32),
                        pltpu.VMEM((6, 128, 128), F32), pltpu.VMEM((2, GROUP, 128), F32),
                        pltpu.SemaphoreType.DMA((3,))],
        compiler_params=params(),
        name="arrive_collide",
    )(lists, index, gathered, before, kinds, absent, *tables)


def last_call(bricks, slots, index, gathered, before, kinds, absent, tables, groups, devices):
    blocks = groups * GROUP * 6
    return pl.pallas_call(
        functools.partial(last_kernel, bricks),
        grid=(groups,),
        in_specs=[SPEC_SMEM, whole(devices, 128), SPEC_POSTED, SPEC_KINDS, SPEC_ABSENT] + [SPEC_ANY] * 3,
        out_specs=SPEC_POPS,
        out_shape=shape_of(19, bricks, SITES),
        scratch_shapes=[pltpu.VMEM((blocks + 2 * slots,) + BLOCK, F32),
                        pltpu.VMEM((18, 128, 128), F32), pltpu.SemaphoreType.DMA((3,))],
        compiler_params=params(),
        name="arrive_out",
    )(index, gathered, before, kinds, absent, *tables)


def share_sums(rows):
    return lax.all_to_all(rows, AXES, 0, 0, tiled=True)


def swap(send, devices):
    even_pairs = [(i, i ^ 1) for i in range(devices)]
    odd_pairs = [(i, i + 1) for i in range(1, devices - 1, 2)]
    odd_pairs = odd_pairs + [(b, a) for a, b in odd_pairs]
    return lax.ppermute(send[0], AXES, even_pairs), lax.ppermute(send[1], AXES, odd_pairs)


def rank(used):
    count = used.shape[0]
    return jnp.sum(jnp.where(iota((count, count), 1) < iota((count, count), 0), used[None, :], 0), axis=1)


def exchange_plan(neighbours, slots, padded):
    bricks = neighbours.shape[0]
    blocks = bricks * 6
    me = lax.axis_index(AXES)
    local = neighbours - me * bricks
    present = neighbours >= 0
    following = present & (local >= bricks)
    preceding = present & (local < 0)
    first = me % 2 == 0
    read = jnp.asarray(np.array(COLUMN_FACE, np.int32))
    given = jnp.asarray(np.array([COLUMN_FACE[OPP[d + 1] - 1] for d in range(18)], np.int32))
    faces = jnp.arange(6, dtype=jnp.int32)
    index = local * 6 + read[None, :]
    lists = []
    for partner in range(2):
        is_next = first if partner == 0 else ~first
        there = jnp.where(is_next, following, preceding)
        spot = (local + jnp.where(is_next, -bricks, bricks)) * 6 + read[None, :]
        used = jnp.any(there[:, :, None] & (given[:, None] == faces[None, :])[None], axis=1)
        used = used.astype(jnp.int32).reshape(-1)
        order = jnp.where(used == 1, rank(used), blocks)
        chosen = order[None, :] == iota((slots, blocks), 0)
        lists.append(jnp.sum(jnp.where(chosen, iota((slots, blocks), 1), 0), axis=1))
        lists.append(jnp.where(jnp.sum(used) > slots, 1, 0)[None])
        flat = jnp.where(there, spot, -1).reshape(-1)
        hits = flat[:, None] == iota((flat.shape[0], blocks), 1)
        ranks = rank(jnp.any(hits, axis=0).astype(jnp.int32))
        at = jnp.sum(jnp.where(hits, jnp.minimum(ranks, slots - 1)[None, :], 0), axis=1)
        index = jnp.where(there, padded * 6 + partner * slots + at.reshape(bricks, 18), index)
    index = jnp.where(present, index, 0)
    index = jnp.pad(index, ((0, padded - bricks), (0, 0))).reshape(-1)
    return jnp.concatenate(lists), index


def begin(devices, slots, populations, neighbours, site_flags, absent):
    bricks = populations.shape[1]
    groups = absent.shape[1] // GROUP
    lists, index = exchange_plan(neighbours, slots, groups * GROUP)
    posted, faces, *send, rows = first_call(lists, populations, site_flags, groups, devices)
    gathered = share_sums(rows)
    sent = swap(send, devices)
    excess = jnp.sum(gathered[:, 127])
    posted, faces, *send, rows = middle_call(
        bricks, lists, index, gathered, posted, site_flags, absent,
        (faces,) + sent, groups, devices)
    gathered = share_sums(rows)
    sent = swap(send, devices)
    return excess, (index, gathered, posted, faces) + sent


def finish(devices, slots, site_flags, absent, bricks, state):
    index, gathered, posted = state[:3]
    return last_call(bricks, slots, index, gathered, posted, site_flags, absent,
                     state[3:], absent.shape[1] // GROUP, devices)


def on_device(devices, populations, neighbours, site_flags):
    bricks = populations.shape[0]
    padded = -(-bricks // GROUP) * GROUP
    absent = jnp.pad((neighbours < 0).astype(jnp.int32), ((0, padded - bricks), (0, 0)))
    absent = jnp.broadcast_to(absent.T[:, :, None], (18, padded, 128))
    populations = jnp.transpose(populations, (1, 0, 2))
    excess, state = begin(devices, SLOTS, populations, neighbours, site_flags, absent)

    def enough(populations, neighbours, state):
        return finish(devices, SLOTS, site_flags, absent, bricks, state)

    def too_few(populations, neighbours, state):
        every = bricks * 6
        _, state = begin(devices, every, populations, neighbours, site_flags, absent)
        return finish(devices, every, site_flags, absent, bricks, state)

    out = lax.cond(excess > 0.0, too_few, enough, populations, neighbours, state)
    return jnp.transpose(out, (1, 0, 2))


def solution(mesh):
    devices = mesh.shape["seg"] * mesh.shape["sub"]
    in_specs = (P(AXES, None, None), P(AXES, None), P(AXES, None))
    return jax.shard_map(
        functools.partial(on_device, devices), mesh=mesh, in_specs=in_specs,
        out_specs=P(AXES, None, None), check_vma=False)
```

```python
import functools

import jax
import jax.numpy as jnp
import numpy as np
from jax import lax
from jax.experimental import pallas as pl
from jax.experimental.pallas import tpu as pltpu
from jax.sharding import PartitionSpec as P

BRICK = 16
PLANE = 256
SITES = 4096
GROUP = 8
CHUNKS = 32
LIMIT = 52
SLOTS = 32
AXES = ("seg", "sub")
INLET = 0.1

SPEEDS = [
    (0, 0, 0),
    (1, 0, 0), (-1, 0, 0), (0, 1, 0), (0, -1, 0), (0, 0, 1), (0, 0, -1),
    (1, 1, 0), (-1, -1, 0), (1, -1, 0), (-1, 1, 0),
    (1, 0, 1), (-1, 0, -1), (1, 0, -1), (-1, 0, 1),
    (0, 1, 1), (0, -1, -1), (0, 1, -1), (0, -1, 1),
]
OPP = [0, 2, 1, 4, 3, 6, 5, 8, 7, 10, 9, 12, 11, 14, 13, 16, 15, 18, 17]


def face_of(speed, dim):
    return 2 * dim + (0 if speed[dim] > 0 else 1)


MEMBERS = [[i for i in range(19) if any(face_of(SPEEDS[i], d) == f and SPEEDS[i][d] for d in range(3))]
           for f in range(6)]
COLUMN_FACE = []
for _d in range(18):
    _m = SPEEDS[OPP[_d + 1]]
    _lead = [k for k in range(3) if _m[k]][0]
    COLUMN_FACE.append(face_of(_m, _lead))
GIVEN = [COLUMN_FACE[OPP[_d + 1] - 1] for _d in range(18)]


def iota(shape, dim):
    return lax.broadcasted_iota(jnp.int32, shape, dim)


def roll(x, shift, axis):
    shift = shift % x.shape[axis]
    return x if shift == 0 else pltpu.roll(x, shift, axis)


def collide(f, kind):
    fluid = kind == 0
    wall = kind == 1
    inlet = kind == 2
    outlet = kind == 3
    even = [f[2 * k + 1] + f[2 * k + 2] for k in range(9)]
    odd = [f[2 * k + 1] - f[2 * k + 2] for k in range(9)]
    density = f[0] + ((even[0] + even[1]) + (even[2] + even[3])) + (
        (even[4] + even[5]) + (even[6] + even[7])) + even[8]
    inverse = 1.0 / density
    ux = (odd[0] + odd[3] + odd[4] + odd[5] + odd[6]) * inverse
    uy = (odd[1] + odd[3] - odd[4] + odd[7] + odd[8]) * inverse
    uz = (odd[2] + odd[5] - odd[6] + odd[7] - odd[8]) * inverse
    ux = jnp.where(inlet, INLET, ux)
    uy = jnp.where(inlet, 0.0, uy)
    uz = jnp.where(inlet, 0.0, uz)
    rho = jnp.where(outlet, 1.0, density)
    base = 1.0 - 1.5 * (ux * ux + uy * uy + uz * uz)
    along = [ux, uy, uz, ux + uy, ux - uy, ux + uz, ux - uz, uy + uz, uy - uz]
    keep_even = jnp.where(fluid, -0.3, jnp.where(wall, 0.5, 0.0))
    take_even = jnp.where(fluid, 0.8, jnp.where(wall, 0.0, 0.5))
    keep_odd = jnp.where(fluid, -0.1, jnp.where(wall, -0.5, 0.0))
    take_odd = jnp.where(fluid, 0.6, jnp.where(wall, 0.0, 0.5))
    fourth = jnp.where(fluid, 0.2 / 12.0, 0.0)
    rho9 = rho * (1.0 / 9.0)
    rho18 = rho * (1.0 / 18.0)
    eq_even = []
    for k in range(9):
        scale = rho9 if k < 3 else rho18
        eq_even.append(scale * (base + 4.5 * along[k] * along[k]))
    eq_rest = (rho * (1.0 / 3.0)) * base
    g_rest = f[0] - eq_rest
    g = [even[k] - eq_even[k] for k in range(9)]
    four = 4.0 * g_rest
    gx, gy, gz = 2.0 * g[0], 2.0 * g[1], 2.0 * g[2]
    ta = four - gx - gy + (g[3] + g[4])
    tb = four - gx - gz + (g[5] + g[6])
    tc = four - gy - gz + (g[7] + g[8])
    shared = (2.0 / 7.0) * (ta + tb + tc)
    ka = (ta - shared) * fourth
    kb = (tb - shared) * fourth
    kc = (tc - shared) * fourth
    kab, kac, kbc = ka + kb, ka + kc, kb + kc
    modes = [-2.0 * kab, -2.0 * kac, -2.0 * kbc, ka, ka, kb, kb, kc, kc]
    odd9 = rho * take_odd * (1.0 / 3.0)
    odd18 = rho * take_odd * (1.0 / 6.0)
    out = [2.0 * (keep_even * f[0] + take_even * eq_rest) + 4.0 * (kab + kc)]
    for k in range(9):
        half_even = keep_even * even[k] + take_even * eq_even[k] + modes[k]
        half_odd = keep_odd * odd[k] + (odd9 if k < 3 else odd18) * along[k]
        out.append(half_even + half_odd)
        out.append(half_even - half_odd)
    return out, density


def side(heading):
    return (15, 0) if heading > 0 else (0, 15)


def slot_of(member, dim):
    return MEMBERS[face_of(SPEEDS[member], dim)].index(member)


def toward(member, dim):
    return 2 * dim + (1 if SPEEDS[member][dim] > 0 else 0)


def pack(value, mark, layers, table, step):
    lane = iota((GROUP, 128), 1)
    for face in range(2):
        leave = 15 if face % 2 == 0 else 0
        for slot, member in enumerate(MEMBERS[face]):
            for h in range(2):
                row = (8 * h + slot) * 8
                layers[face, row:row + 8, :] = value(member, 2 * leave + h)
        for h in range(2):
            row = (8 * h + 5) * 8
            layers[face, row:row + 8, :] = mark(2 * leave + h)

    def line(x, carry):
        rows = pl.ds(pl.multiple_of(8 * x, 8), 8)
        outlet = [mark(2 * x + h) for h in range(2)]
        for face in range(2, 6):
            leave = 15 if face % 2 == 0 else 0
            packed = None
            for slot, member in enumerate(MEMBERS[face] + [None]):
                if face < 4:
                    piece = outlet[leave // 8] if member is None else value(member, 2 * x + leave // 8)
                    piece = roll(piece, 16 * slot - 16 * (leave % 8), 1)
                    packed = piece if packed is None else jnp.where((lane >> 4) == slot, piece, packed)
                else:
                    for h in range(2):
                        piece = outlet[h] if member is None else value(member, 2 * x + h)
                        piece = roll(piece, 8 * h + slot - leave, 1)
                        packed = (piece if packed is None
                                  else jnp.where((lane & 15) == 8 * h + slot, piece, packed))
            layers[face, rows, :] = packed
        return carry

    lax.fori_loop(0, BRICK, line, 0, unroll=4)
    unpack(layers, table, step)


def unpack(layers, table, step):
    for face in range(6):
        for j in range(GROUP):
            table[(step * GROUP + j) * 6 + face] = layers[face, pl.ds(j, BRICK, stride=8), :]


def scaled(block, face, mean):
    if face < 2:
        parts = []
        for h in range(2):
            part = block[8 * h:8 * h + 8, :]
            parts.append(jnp.where(jnp.broadcast_to(part[5:6, :], (8, 128)) != 0.0, part * mean, part))
        return jnp.concatenate(parts, axis=0)
    lane = iota(BLOCK, 1)
    by = 16 if face < 4 else 1
    slot = jnp.minimum(lane >> 4, 5) if face < 4 else jnp.minimum(lane & 7, 5)
    marks = jnp.take_along_axis(block, lane + (5 - slot) * by, axis=1, mode="promise_in_bounds")
    return jnp.where((slot < 5) & (marks != 0.0), block * jnp.concatenate([mean, mean], axis=0), block)


def gather(bricks, index, step, gathered, table, mean, arriving):
    me = index[index.shape[0] - 1]
    near = jnp.abs(iota(gathered.shape, 0) - me) <= 1
    outlets = jnp.max(jnp.where(near & (iota(gathered.shape, 1) == 126), gathered[...], 0.0))
    real = jnp.minimum(GROUP, bricks - step * GROUP)

    def fetch(scale):
        def brick(j, carry):
            base = (step * GROUP + j) * 18
            for column in range(18):
                block = scale(table[index[base + column]], COLUMN_FACE[column])
                arriving[column, pl.ds(j, BRICK, stride=8), :] = block
            return carry

        lax.fori_loop(0, real, brick, 0)

    @pl.when(outlets > 0.0)
    def _():
        fetch(lambda block, face: scaled(block, face, mean))

    @pl.when(outlets == 0.0)
    def _():
        fetch(lambda block, face: block)


def stream(posted, kinds, absent, arriving, mean, put):
    lane = iota((GROUP, 128), 1)

    def scale(chunk):
        lanes = pl.ds(pl.multiple_of(128 * chunk, 128), 128)
        return jnp.where(kinds[:, lanes] == 3, mean, 1.0)

    def line(x, carry):
        before = (x + 15) & 15
        after = (x + 1) & 15
        place = {0: x, 1: before, -1: after}
        scales = {cx: (scale(2 * place[cx]), scale(2 * place[cx] + 1)) for cx in (0, 1, -1)}

        for member in range(19):
            if member % 2 == 1 or member == 0:
                loaded = {}

            def load(member, cx, h):
                if (member, cx, h) not in loaded:
                    loaded[member, cx, h] = posted[0, member, 2 * place[cx] + h] * scales[cx][h]
                return loaded[member, cx, h]

            cx, cy, cz = SPEEDS[member]
            parts = [load(member, cx, h) for h in range(2)]
            mirror = [None, None]
            if cy or cz:
                mirror = [load(OPP[member], 0, h) for h in range(2)]
            if cy:
                by = 16 * cy + cz
                first, second = roll(parts[0], by, 1), roll(parts[1], by, 1)
                carried = lane < by if cy > 0 else lane >= 128 + by
                parts = [jnp.where(carried, second, first), jnp.where(carried, first, second)]
            elif cz:
                parts = [roll(part, cz, 1) for part in parts]
            rows = pl.ds(pl.multiple_of(8 * place[cx], 8), 8)
            if cy:
                leave, enter = side(cy)
                column = toward(member, 1)
                half = enter // 8
                shift = 16 * (enter % 8) - 16 * slot_of(member, 1)
                here = (lane >> 4) == enter % 8
                new = roll(arriving[column, rows, :], shift + cz, 1)
                new = jnp.where(absent[column] != 0, mirror[half], new)
                parts[half] = jnp.where(here, new, parts[half])
            if cz:
                leave, enter = side(cz)
                column = toward(member, 2)
                slot = slot_of(member, 2)
                gone = absent[column] != 0
                here = (lane & 15) == enter
                block = arriving[column, rows, :]
                for h in range(2):
                    if cy and h == (1 if cy > 0 else 0):
                        half_of = jnp.where(lane < 16 if cy > 0 else lane >= 112, 1 - h, h)
                        origin = ((lane - 16 * cy) & 112) + slot + 8 * half_of
                        new = jnp.take_along_axis(block, origin, axis=1, mode="promise_in_bounds")
                    else:
                        new = roll(block, 16 * cy + enter - slot - 8 * h, 1)
                    new = jnp.where(gone, mirror[h], new)
                    parts[h] = jnp.where(here, new, parts[h])
            if cy and cz:
                leave, enter = side(cy)
                column = OPP[member] - 1
                half = enter // 8
                shift = 16 * (enter % 8) - 16 * slot_of(member, 1)
                corner = ((lane >> 4) == enter % 8) & ((lane & 15) == side(cz)[1])
                new = roll(arriving[column, rows, :], shift - 15 * cz, 1)
                new = jnp.where(absent[column] != 0, mirror[half], new)
                parts[half] = jnp.where(corner, new, parts[half])
            for h in range(2):
                put(member, 2 * x + h, parts[h])
        return carry

    lax.fori_loop(0, BRICK, line, 0, unroll=2)

    for member in range(19):
        cx, cy, cz = SPEEDS[member]
        if not cx:
            continue
        leave, enter = side(cx)
        slot = slot_of(member, 0)
        mirror = [posted[0, OPP[member], 2 * enter + h] * scale(2 * enter + h) for h in range(2)]

        def plane(column):
            parts = []
            for h in range(2):
                row = (8 * h + slot) * 8
                parts.append(arriving[column, row:row + 8, :])
            if cy:
                first, second = roll(parts[0], 16 * cy, 1), roll(parts[1], 16 * cy, 1)
                carried = lane < 16 if cy > 0 else lane >= 112
                parts = [jnp.where(carried, second, first), jnp.where(carried, first, second)]
            return [jnp.where(absent[column] != 0, mirror[h], parts[h]) for h in range(2)]

        def edge_plane(column):
            if cy:
                return plane(column)
            parts = []
            for h in range(2):
                row = (8 * h + slot) * 8
                parts.append(roll(arriving[column, row:row + 8, :], -15 * cz, 1))
            return [jnp.where(absent[column] != 0, mirror[h], parts[h]) for h in range(2)]

        parts = plane(toward(member, 0))
        if cz:
            column = toward(member, 0)
            parts = []
            for h in range(2):
                row = (8 * h + slot) * 8
                new = roll(arriving[column, row:row + 8, :], cz, 1)
                parts.append(jnp.where(absent[column] != 0, mirror[h], new))
        if cy or cz:
            edges = edge_plane(OPP[member] - 1)
            for h in range(2):
                if cy:
                    if side(cy)[1] // 8 != h:
                        continue
                    corner = (lane >> 4) == side(cy)[1] % 8
                else:
                    corner = (lane & 15) == side(cz)[1]
                parts[h] = jnp.where(corner, edges[h], parts[h])
        for h in range(2):
            put(member, 2 * enter + h, parts[h])


def mean_of(gathered):
    total = jnp.sum(gathered[...], axis=0, keepdims=True)
    ratio = total / pltpu.roll(total, 64, 1)
    return jnp.broadcast_to(ratio[:, 0:1], (GROUP, 128))


def collide_all(load, kinds, posted, sums, rows_out, step, bricks, excess):
    real = iota((GROUP, 128), 0) + step * GROUP < bricks

    def chunk(c, carry):
        lanes = pl.ds(pl.multiple_of(128 * c, 128), 128)
        kind = kinds[:, lanes]
        out, density = collide([load(i, c) for i in range(19)], kind)
        for i in range(19):
            posted[0, i, c] = out[i]
        counted = real & (kind != 1)
        return (carry[0] + jnp.where(counted, density, 0.0),
                carry[1] + jnp.where(counted, 1.0, 0.0),
                carry[2] + jnp.where(real & (kind == 3), 1.0, 0.0))

    zero = jnp.zeros((GROUP, 128), F32)
    total = lax.fori_loop(0, CHUNKS, chunk, (zero, zero, zero), unroll=4)

    @pl.when(step == 0)
    def _():
        for k in range(3):
            sums[k] = total[k]

    @pl.when(step > 0)
    def _():
        for k in range(3):
            sums[k] += total[k]

    @pl.when(step == pl.num_programs(0) - 1)
    def _():
        lane = iota(rows_out.shape, 1)
        both = jnp.where(lane < 64, jnp.sum(sums[0]), jnp.sum(sums[1]))
        both = jnp.where(lane == 126, jnp.sum(sums[2]), both)
        rows_out[...] = jnp.where(lane == 127, excess, both)


def plan_sends(neighbours, me, lists):
    bricks = neighbours.shape[0]
    low = me * bricks
    high = low + bricks
    following = (me & 1) * 128
    preceding = 128 - following

    def brick(b, counts):
        ahead, behind = counts
        near = [neighbours[b, c] for c in range(18)]
        held = [jnp.where(v < 0, 1 << 30, v) for v in near]
        for face in range(6):
            columns = [c for c in range(18) if GIVEN[c] == face]
            last = functools.reduce(jnp.maximum, [near[c] for c in columns])
            first = functools.reduce(jnp.minimum, [held[c] for c in columns])
            lists[following + ahead] = b * 6 + face
            lists[preceding + behind] = b * 6 + face
            ahead += jnp.where(last >= high, 1, 0)
            behind += jnp.where(first < low, 1, 0)
        return ahead, behind

    ahead, behind = lax.fori_loop(0, bricks, brick, (jnp.int32(0), jnp.int32(0)))
    lists[following + 127] = ahead
    lists[preceding + 127] = behind


def select_blocks(lists, table, send):
    slots = send[0].shape[0]

    @pl.when(pl.program_id(0) == pl.num_programs(0) - 1)
    def _():
        def slot(s, carry):
            for partner in range(2):
                listed = s < lists[128 * partner + 127]
                send[partner][s] = table[jnp.where(listed, lists[128 * partner + s], 0)]
            return carry

        lax.fori_loop(0, slots, slot, 0, unroll=4)


def outlet_mark(kinds):
    def mark(chunk):
        start = 128 * chunk
        if not isinstance(start, int):
            start = pl.multiple_of(start, 128)
        return jnp.where(kinds[:, pl.ds(start, 128)] == 3, 1.0, 0.0)

    return mark


def first_kernel(bricks, me, neighbours, pops, kinds, posted, faces, send_even, send_odd, rows_out, lists,
                 layers, sums):
    step = pl.program_id(0)
    slots = send_even.shape[0]

    @pl.when(step == 0)
    def _():
        plan_sends(neighbours, me[0], lists)

    excess = jnp.where(jnp.maximum(lists[127], lists[255]) > slots, 1.0, 0.0)

    def load(i, c):
        return pops[i, :, pl.ds(pl.multiple_of(128 * c, 128), 128)]

    collide_all(load, kinds, posted, sums, rows_out, step, bricks, excess)
    pack(lambda m, c: posted[0, m, c], outlet_mark(kinds), layers, faces, step)
    select_blocks(lists, faces, (send_even, send_odd))


def take_table(pieces, table, sems):
    copies = []
    start = 0
    for k, piece in enumerate(pieces):
        count = piece.shape[0]
        copies.append(pltpu.make_async_copy(piece, table.at[pl.ds(start, count)], sems.at[k]))
        start += count
    for copy in copies:
        copy.start()
    for copy in copies:
        copy.wait()


def middle_kernel(bricks, lists, index, gathered, before, kinds, absent, own, even, odd,
                  posted, faces, send_even, send_odd, rows_out, table, arriving, pops, layers, sums, sems):
    step = pl.program_id(0)

    @pl.when(step == 0)
    def _():
        take_table((own, even, odd), table, sems)

    mean = mean_of(gathered)
    gather(bricks, index, step, gathered, table, mean, arriving)

    def put(member, chunk, value):
        pops[member, chunk] = value

    stream(before, kinds, absent, arriving, mean, put)
    collide_all(lambda i, c: pops[i, c], kinds, posted, sums, rows_out, step, bricks, 0.0)
    pack(lambda m, c: posted[0, m, c], outlet_mark(kinds), layers, faces, step)
    select_blocks(lists, faces, (send_even, send_odd))


def last_kernel(bricks, index, gathered, before, kinds, absent, own, even, odd, out, table, arriving, sems):
    step = pl.program_id(0)

    @pl.when(step == 0)
    def _():
        take_table((own, even, odd), table, sems)

    mean = mean_of(gathered)
    gather(bricks, index, step, gathered, table, mean, arriving)

    def put(member, chunk, value):
        start = 128 * chunk
        if not isinstance(start, int):
            start = pl.multiple_of(start, 128)
        out[member, :, pl.ds(start, 128)] = value

    stream(before, kinds, absent, arriving, mean, put)


F32 = jnp.float32
BLOCK = (BRICK, 128)
POSTED = (19, CHUNKS, GROUP, 128)


def params():
    return pltpu.CompilerParams(
        dimension_semantics=("arbitrary",), vmem_limit_bytes=LIMIT * 1024 * 1024)


def whole(*shape):
    return pl.BlockSpec(shape, lambda i: (0,) * len(shape))


SPEC_POPS = pl.BlockSpec((19, GROUP, SITES), lambda i: (0, i, 0))
SPEC_KINDS = pl.BlockSpec((GROUP, SITES), lambda i: (i, 0))
SPEC_POSTED = pl.BlockSpec((1,) + POSTED, lambda i: (i, 0, 0, 0, 0))
SPEC_ABSENT = pl.BlockSpec((18, GROUP, 128), lambda i: (0, i, 0))
SPEC_SMEM = pl.BlockSpec(memory_space=pltpu.SMEM)
SPEC_ANY = pl.BlockSpec(memory_space=pl.ANY)


def shape_of(*shape):
    return jax.ShapeDtypeStruct(shape, F32)


def first_call(slots, me, neighbours, pops, kinds, groups, devices):
    blocks = groups * GROUP * 6
    return pl.pallas_call(
        functools.partial(first_kernel, pops.shape[1]),
        grid=(groups,),
        in_specs=[SPEC_SMEM, SPEC_SMEM, SPEC_POPS, SPEC_KINDS],
        out_specs=[SPEC_POSTED, whole(blocks, *BLOCK), whole(slots, *BLOCK), whole(slots, *BLOCK),
                   whole(devices, 128), SPEC_SMEM],
        out_shape=[shape_of(groups, *POSTED), pltpu.HBM((blocks,) + BLOCK, F32), shape_of(slots, *BLOCK),
                   shape_of(slots, *BLOCK), shape_of(devices, 128),
                   jax.ShapeDtypeStruct((256,), jnp.int32)],
        scratch_shapes=[pltpu.VMEM((6, 128, 128), F32), pltpu.VMEM((3, GROUP, 128), F32)],
        compiler_params=params(),
        name="first_collide",
    )(me, neighbours, pops, kinds)


def middle_call(bricks, slots, lists, index, gathered, before, kinds, absent, tables, groups, devices):
    blocks = groups * GROUP * 6
    return pl.pallas_call(
        functools.partial(middle_kernel, bricks),
        grid=(groups,),
        in_specs=[SPEC_SMEM, SPEC_SMEM, whole(devices, 128), SPEC_POSTED, SPEC_KINDS,
                  SPEC_ABSENT] + [SPEC_ANY] * 3,
        out_specs=[SPEC_POSTED, whole(blocks, *BLOCK), whole(slots, *BLOCK), whole(slots, *BLOCK),
                   whole(devices, 128)],
        out_shape=[shape_of(groups, *POSTED), pltpu.HBM((blocks,) + BLOCK, F32), shape_of(slots, *BLOCK),
                   shape_of(slots, *BLOCK), shape_of(devices, 128)],
        scratch_shapes=[pltpu.VMEM((blocks + 2 * slots,) + BLOCK, F32),
                        pltpu.VMEM((18, 128, 128), F32), pltpu.VMEM(POSTED, F32),
                        pltpu.VMEM((6, 128, 128), F32), pltpu.VMEM((3, GROUP, 128), F32),
                        pltpu.SemaphoreType.DMA((3,))],
        compiler_params=params(),
        name="arrive_collide",
    )(lists, index, gathered, before, kinds, absent, *tables)


def last_call(bricks, slots, index, gathered, before, kinds, absent, tables, groups, devices):
    blocks = groups * GROUP * 6
    return pl.pallas_call(
        functools.partial(last_kernel, bricks),
        grid=(groups,),
        in_specs=[SPEC_SMEM, whole(devices, 128), SPEC_POSTED, SPEC_KINDS, SPEC_ABSENT] + [SPEC_ANY] * 3,
        out_specs=SPEC_POPS,
        out_shape=shape_of(19, bricks, SITES),
        scratch_shapes=[pltpu.VMEM((blocks + 2 * slots,) + BLOCK, F32),
                        pltpu.VMEM((18, 128, 128), F32), pltpu.SemaphoreType.DMA((3,))],
        compiler_params=params(),
        name="arrive_out",
    )(index, gathered, before, kinds, absent, *tables)


def share_sums(rows):
    return lax.all_to_all(rows, AXES, 0, 0, tiled=True)


def swap(send, devices):
    even_pairs = [(i, i ^ 1) for i in range(devices)]
    odd_pairs = [(i, i + 1) for i in range(1, devices - 1, 2)]
    odd_pairs = odd_pairs + [(b, a) for a, b in odd_pairs]
    return lax.ppermute(send[0], AXES, even_pairs), lax.ppermute(send[1], AXES, odd_pairs)


def rank(used):
    count = used.shape[0]
    return jnp.sum(jnp.where(iota((count, count), 1) < iota((count, count), 0), used[None, :], 0), axis=1)


def arrival_plan(neighbours, slots, padded):
    bricks = neighbours.shape[0]
    blocks = bricks * 6
    me = lax.axis_index(AXES)
    local = neighbours - me * bricks
    present = neighbours >= 0
    following = present & (local >= bricks)
    preceding = present & (local < 0)
    first = me % 2 == 0
    read = jnp.asarray(np.array(COLUMN_FACE, np.int32))
    index = local * 6 + read[None, :]
    for partner in range(2):
        is_next = first if partner == 0 else ~first
        there = jnp.where(is_next, following, preceding)
        spot = (local + jnp.where(is_next, -bricks, bricks)) * 6 + read[None, :]
        flat = jnp.where(there, spot, -1).reshape(-1)
        hits = flat[:, None] == iota((flat.shape[0], blocks), 1)
        ranks = rank(jnp.any(hits, axis=0).astype(jnp.int32))
        at = jnp.sum(jnp.where(hits, jnp.minimum(ranks, slots - 1)[None, :], 0), axis=1)
        index = jnp.where(there, padded * 6 + partner * slots + at.reshape(bricks, 18), index)
    index = jnp.where(present, index, 0)
    index = jnp.pad(index, ((0, padded - bricks), (0, 0))).reshape(-1)
    return jnp.concatenate([index, me[None]])


def begin(devices, slots, populations, neighbours, site_flags, absent):
    bricks = populations.shape[1]
    groups = absent.shape[1] // GROUP
    me = lax.axis_index(AXES).astype(jnp.int32).reshape(1)
    index = arrival_plan(neighbours, slots, groups * GROUP)
    posted, faces, *send, rows, lists = first_call(
        slots, me, neighbours, populations, site_flags, groups, devices)
    gathered = share_sums(rows)
    sent = swap(send, devices)
    excess = jnp.sum(gathered[:, 127])
    posted, faces, *send, rows = middle_call(
        bricks, slots, lists, index, gathered, posted, site_flags, absent,
        (faces,) + sent, groups, devices)
    gathered = share_sums(rows)
    sent = swap(send, devices)
    return excess, (index, gathered, posted, faces) + sent


def finish(devices, slots, site_flags, absent, bricks, state):
    index, gathered, posted = state[:3]
    return last_call(bricks, slots, index, gathered, posted, site_flags, absent,
                     state[3:], absent.shape[1] // GROUP, devices)


def on_device(devices, populations, neighbours, site_flags):
    bricks = populations.shape[0]
    padded = -(-bricks // GROUP) * GROUP
    absent = jnp.pad((neighbours < 0).astype(jnp.int32), ((0, padded - bricks), (0, 0)))
    absent = jnp.broadcast_to(absent.T[:, :, None], (18, padded, 128))
    populations = jnp.transpose(populations, (1, 0, 2))
    excess, state = begin(devices, SLOTS, populations, neighbours, site_flags, absent)

    def enough(populations, neighbours, state):
        return finish(devices, SLOTS, site_flags, absent, bricks, state)

    def too_few(populations, neighbours, state):
        every = bricks * 6
        _, state = begin(devices, every, populations, neighbours, site_flags, absent)
        return finish(devices, every, site_flags, absent, bricks, state)

    out = lax.cond(excess > 0.0, too_few, enough, populations, neighbours, state)
    return jnp.transpose(out, (1, 0, 2))


def solution(mesh):
    devices = mesh.shape["seg"] * mesh.shape["sub"]
    in_specs = (P(AXES, None, None), P(AXES, None), P(AXES, None))
    return jax.shard_map(
        functools.partial(on_device, devices), mesh=mesh, in_specs=in_specs,
        out_specs=P(AXES, None, None), check_vma=False)
```

```python
import functools

import jax
import jax.numpy as jnp
import numpy as np
from jax import lax
from jax.experimental import pallas as pl
from jax.experimental.pallas import tpu as pltpu
from jax.sharding import PartitionSpec as P

BRICK = 16
PLANE = 256
SITES = 4096
GROUP = 8
CHUNKS = 32
AT_ONCE = 4
LIMIT = 52
SLOTS = 32
AXES = ("seg", "sub")
INLET = 0.1

SPEEDS = [
    (0, 0, 0),
    (1, 0, 0), (-1, 0, 0), (0, 1, 0), (0, -1, 0), (0, 0, 1), (0, 0, -1),
    (1, 1, 0), (-1, -1, 0), (1, -1, 0), (-1, 1, 0),
    (1, 0, 1), (-1, 0, -1), (1, 0, -1), (-1, 0, 1),
    (0, 1, 1), (0, -1, -1), (0, 1, -1), (0, -1, 1),
]
OPP = [0, 2, 1, 4, 3, 6, 5, 8, 7, 10, 9, 12, 11, 14, 13, 16, 15, 18, 17]


def face_of(speed, dim):
    return 2 * dim + (0 if speed[dim] > 0 else 1)


MEMBERS = [[i for i in range(19) if any(face_of(SPEEDS[i], d) == f and SPEEDS[i][d] for d in range(3))]
           for f in range(6)]
COLUMN_FACE = []
for _d in range(18):
    _m = SPEEDS[OPP[_d + 1]]
    _lead = [k for k in range(3) if _m[k]][0]
    COLUMN_FACE.append(face_of(_m, _lead))
GIVEN = [COLUMN_FACE[OPP[_d + 1] - 1] for _d in range(18)]


def iota(shape, dim):
    return lax.broadcasted_iota(jnp.int32, shape, dim)


def roll(x, shift, axis):
    shift = shift % x.shape[axis]
    return x if shift == 0 else pltpu.roll(x, shift, axis)


def collide(f, kind):
    fluid = kind == 0
    wall = kind == 1
    inlet = kind == 2
    outlet = kind == 3
    even = [f[2 * k + 1] + f[2 * k + 2] for k in range(9)]
    odd = [f[2 * k + 1] - f[2 * k + 2] for k in range(9)]
    density = f[0] + ((even[0] + even[1]) + (even[2] + even[3])) + (
        (even[4] + even[5]) + (even[6] + even[7])) + even[8]
    inverse = 1.0 / density
    ux = (odd[0] + odd[3] + odd[4] + odd[5] + odd[6]) * inverse
    uy = (odd[1] + odd[3] - odd[4] + odd[7] + odd[8]) * inverse
    uz = (odd[2] + odd[5] - odd[6] + odd[7] - odd[8]) * inverse
    ux = jnp.where(inlet, INLET, ux)
    uy = jnp.where(inlet, 0.0, uy)
    uz = jnp.where(inlet, 0.0, uz)
    rho = jnp.where(outlet, 1.0, density)
    base = 1.0 - 1.5 * (ux * ux + uy * uy + uz * uz)
    along = [ux, uy, uz, ux + uy, ux - uy, ux + uz, ux - uz, uy + uz, uy - uz]
    keep_even = jnp.where(fluid, -0.3, jnp.where(wall, 0.5, 0.0))
    take_even = jnp.where(fluid, 0.8, jnp.where(wall, 0.0, 0.5))
    keep_odd = jnp.where(fluid, -0.1, jnp.where(wall, -0.5, 0.0))
    take_odd = jnp.where(fluid, 0.6, jnp.where(wall, 0.0, 0.5))
    fourth = jnp.where(fluid, 0.2 / 12.0, 0.0)
    rho9 = rho * (1.0 / 9.0)
    rho18 = rho * (1.0 / 18.0)
    eq_even = []
    for k in range(9):
        scale = rho9 if k < 3 else rho18
        eq_even.append(scale * (base + 4.5 * along[k] * along[k]))
    eq_rest = (rho * (1.0 / 3.0)) * base
    g_rest = f[0] - eq_rest
    g = [even[k] - eq_even[k] for k in range(9)]
    four = 4.0 * g_rest
    gx, gy, gz = 2.0 * g[0], 2.0 * g[1], 2.0 * g[2]
    ta = four - gx - gy + (g[3] + g[4])
    tb = four - gx - gz + (g[5] + g[6])
    tc = four - gy - gz + (g[7] + g[8])
    shared = (2.0 / 7.0) * (ta + tb + tc)
    ka = (ta - shared) * fourth
    kb = (tb - shared) * fourth
    kc = (tc - shared) * fourth
    kab, kac, kbc = ka + kb, ka + kc, kb + kc
    modes = [-2.0 * kab, -2.0 * kac, -2.0 * kbc, ka, ka, kb, kb, kc, kc]
    odd9 = rho * take_odd * (1.0 / 3.0)
    odd18 = rho * take_odd * (1.0 / 6.0)
    out = [2.0 * (keep_even * f[0] + take_even * eq_rest) + 4.0 * (kab + kc)]
    for k in range(9):
        half_even = keep_even * even[k] + take_even * eq_even[k] + modes[k]
        half_odd = keep_odd * odd[k] + (odd9 if k < 3 else odd18) * along[k]
        out.append(half_even + half_odd)
        out.append(half_even - half_odd)
    return out, density


def side(heading):
    return (15, 0) if heading > 0 else (0, 15)


def slot_of(member, dim):
    return MEMBERS[face_of(SPEEDS[member], dim)].index(member)


def toward(member, dim):
    return 2 * dim + (1 if SPEEDS[member][dim] > 0 else 0)


def pack(value, mark, layers, table, step):
    lane = iota((GROUP, 128), 1)
    for face in range(2):
        leave = 15 if face % 2 == 0 else 0
        for slot, member in enumerate(MEMBERS[face]):
            for h in range(2):
                row = (8 * h + slot) * 8
                layers[face, row:row + 8, :] = value(member, 2 * leave + h)
        for h in range(2):
            row = (8 * h + 5) * 8
            layers[face, row:row + 8, :] = mark(2 * leave + h)

    def line(x, carry):
        rows = pl.ds(pl.multiple_of(8 * x, 8), 8)
        outlet = [mark(2 * x + h) for h in range(2)]
        for face in range(2, 6):
            leave = 15 if face % 2 == 0 else 0
            packed = None
            for slot, member in enumerate(MEMBERS[face] + [None]):
                if face < 4:
                    piece = outlet[leave // 8] if member is None else value(member, 2 * x + leave // 8)
                    piece = roll(piece, 16 * slot - 16 * (leave % 8), 1)
                    packed = piece if packed is None else jnp.where((lane >> 4) == slot, piece, packed)
                else:
                    for h in range(2):
                        piece = outlet[h] if member is None else value(member, 2 * x + h)
                        piece = roll(piece, 8 * h + slot - leave, 1)
                        packed = (piece if packed is None
                                  else jnp.where((lane & 15) == 8 * h + slot, piece, packed))
            layers[face, rows, :] = packed
        return carry

    lax.fori_loop(0, BRICK, line, 0, unroll=8)
    unpack(layers, table, step)


def unpack(layers, table, step):
    for face in range(6):
        for j in range(GROUP):
            table[(step * GROUP + j) * 6 + face] = layers[face, pl.ds(j, BRICK, stride=8), :]


def scaled(block, face, mean):
    if face < 2:
        parts = []
        for h in range(2):
            part = block[8 * h:8 * h + 8, :]
            parts.append(jnp.where(jnp.broadcast_to(part[5:6, :], (8, 128)) != 0.0, part * mean, part))
        return jnp.concatenate(parts, axis=0)
    lane = iota(BLOCK, 1)
    by = 16 if face < 4 else 1
    slot = jnp.minimum(lane >> 4, 5) if face < 4 else jnp.minimum(lane & 7, 5)
    marks = jnp.take_along_axis(block, lane + (5 - slot) * by, axis=1, mode="promise_in_bounds")
    return jnp.where((slot < 5) & (marks != 0.0), block * jnp.concatenate([mean, mean], axis=0), block)


def gather(bricks, index, step, gathered, table, mean, arriving):
    me = index[index.shape[0] - 1]
    near = jnp.abs(iota(gathered.shape, 0) - me) <= 1
    outlets = jnp.max(jnp.where(near & (iota(gathered.shape, 1) == 126), gathered[...], 0.0))
    real = jnp.minimum(GROUP, bricks - step * GROUP)

    def fetch(scale):
        def some(k, carry):
            for i in range(AT_ONCE):
                j = k * AT_ONCE + i
                base = (step * GROUP + j) * 18
                for column in range(18):
                    block = scale(table[index[base + column]], COLUMN_FACE[column])
                    arriving[column, pl.ds(j, BRICK, stride=8), :] = block
            return carry

        lax.fori_loop(0, (real + AT_ONCE - 1) // AT_ONCE, some, 0)

    @pl.when(outlets > 0.0)
    def _():
        fetch(lambda block, face: scaled(block, face, mean))

    @pl.when(outlets == 0.0)
    def _():
        fetch(lambda block, face: block)


def stream(posted, kinds, absent, arriving, mean, put):
    lane = iota((GROUP, 128), 1)

    def scale(chunk):
        lanes = pl.ds(pl.multiple_of(128 * chunk, 128), 128)
        return jnp.where(kinds[:, lanes] == 3, mean, 1.0)

    def line(x, carry):
        before = (x + 15) & 15
        after = (x + 1) & 15
        place = {0: x, 1: before, -1: after}
        scales = {cx: (scale(2 * place[cx]), scale(2 * place[cx] + 1)) for cx in (0, 1, -1)}

        for member in range(19):
            if member % 2 == 1 or member == 0:
                loaded = {}

            def load(member, cx, h):
                if (member, cx, h) not in loaded:
                    loaded[member, cx, h] = posted[0, member, 2 * place[cx] + h] * scales[cx][h]
                return loaded[member, cx, h]

            cx, cy, cz = SPEEDS[member]
            parts = [load(member, cx, h) for h in range(2)]
            mirror = [None, None]
            if cy or cz:
                mirror = [load(OPP[member], 0, h) for h in range(2)]
            if cy:
                by = 16 * cy + cz
                first, second = roll(parts[0], by, 1), roll(parts[1], by, 1)
                carried = lane < by if cy > 0 else lane >= 128 + by
                parts = [jnp.where(carried, second, first), jnp.where(carried, first, second)]
            elif cz:
                parts = [roll(part, cz, 1) for part in parts]
            rows = pl.ds(pl.multiple_of(8 * place[cx], 8), 8)
            if cy:
                leave, enter = side(cy)
                column = toward(member, 1)
                half = enter // 8
                shift = 16 * (enter % 8) - 16 * slot_of(member, 1)
                here = (lane >> 4) == enter % 8
                new = roll(arriving[column, rows, :], shift + cz, 1)
                new = jnp.where(absent[column] != 0, mirror[half], new)
                parts[half] = jnp.where(here, new, parts[half])
            if cz:
                leave, enter = side(cz)
                column = toward(member, 2)
                slot = slot_of(member, 2)
                gone = absent[column] != 0
                here = (lane & 15) == enter
                block = arriving[column, rows, :]
                for h in range(2):
                    if cy and h == (1 if cy > 0 else 0):
                        half_of = jnp.where(lane < 16 if cy > 0 else lane >= 112, 1 - h, h)
                        origin = ((lane - 16 * cy) & 112) + slot + 8 * half_of
                        new = jnp.take_along_axis(block, origin, axis=1, mode="promise_in_bounds")
                    else:
                        new = roll(block, 16 * cy + enter - slot - 8 * h, 1)
                    new = jnp.where(gone, mirror[h], new)
                    parts[h] = jnp.where(here, new, parts[h])
            if cy and cz:
                leave, enter = side(cy)
                column = OPP[member] - 1
                half = enter // 8
                shift = 16 * (enter % 8) - 16 * slot_of(member, 1)
                corner = ((lane >> 4) == enter % 8) & ((lane & 15) == side(cz)[1])
                new = roll(arriving[column, rows, :], shift - 15 * cz, 1)
                new = jnp.where(absent[column] != 0, mirror[half], new)
                parts[half] = jnp.where(corner, new, parts[half])
            for h in range(2):
                put(member, 2 * x + h, parts[h])
        return carry

    lax.fori_loop(0, BRICK, line, 0, unroll=4)

    for member in range(19):
        cx, cy, cz = SPEEDS[member]
        if not cx:
            continue
        leave, enter = side(cx)
        slot = slot_of(member, 0)
        mirror = [posted[0, OPP[member], 2 * enter + h] * scale(2 * enter + h) for h in range(2)]

        def plane(column):
            parts = []
            for h in range(2):
                row = (8 * h + slot) * 8
                parts.append(arriving[column, row:row + 8, :])
            if cy:
                first, second = roll(parts[0], 16 * cy, 1), roll(parts[1], 16 * cy, 1)
                carried = lane < 16 if cy > 0 else lane >= 112
                parts = [jnp.where(carried, second, first), jnp.where(carried, first, second)]
            return [jnp.where(absent[column] != 0, mirror[h], parts[h]) for h in range(2)]

        def edge_plane(column):
            if cy:
                return plane(column)
            parts = []
            for h in range(2):
                row = (8 * h + slot) * 8
                parts.append(roll(arriving[column, row:row + 8, :], -15 * cz, 1))
            return [jnp.where(absent[column] != 0, mirror[h], parts[h]) for h in range(2)]

        parts = plane(toward(member, 0))
        if cz:
            column = toward(member, 0)
            parts = []
            for h in range(2):
                row = (8 * h + slot) * 8
                new = roll(arriving[column, row:row + 8, :], cz, 1)
                parts.append(jnp.where(absent[column] != 0, mirror[h], new))
        if cy or cz:
            edges = edge_plane(OPP[member] - 1)
            for h in range(2):
                if cy:
                    if side(cy)[1] // 8 != h:
                        continue
                    corner = (lane >> 4) == side(cy)[1] % 8
                else:
                    corner = (lane & 15) == side(cz)[1]
                parts[h] = jnp.where(corner, edges[h], parts[h])
        for h in range(2):
            put(member, 2 * enter + h, parts[h])


def mean_of(gathered):
    total = jnp.sum(gathered[...], axis=0, keepdims=True)
    ratio = total / pltpu.roll(total, 64, 1)
    return jnp.broadcast_to(ratio[:, 0:1], (GROUP, 128))


def collide_all(load, kinds, posted, sums, rows_out, step, bricks, excess):
    real = iota((GROUP, 128), 0) + step * GROUP < bricks

    def chunk(c, carry):
        lanes = pl.ds(pl.multiple_of(128 * c, 128), 128)
        kind = kinds[:, lanes]
        out, density = collide([load(i, c) for i in range(19)], kind)
        for i in range(19):
            posted[0, i, c] = out[i]
        counted = real & (kind != 1)
        return (carry[0] + jnp.where(counted, density, 0.0),
                carry[1] + jnp.where(counted, 1.0, 0.0),
                carry[2] + jnp.where(real & (kind == 3), 1.0, 0.0))

    zero = jnp.zeros((GROUP, 128), F32)
    total = lax.fori_loop(0, CHUNKS, chunk, (zero, zero, zero), unroll=8)

    @pl.when(step == 0)
    def _():
        for k in range(3):
            sums[k] = total[k]

    @pl.when(step > 0)
    def _():
        for k in range(3):
            sums[k] += total[k]

    @pl.when(step == pl.num_programs(0) - 1)
    def _():
        lane = iota(rows_out.shape, 1)
        both = jnp.where(lane < 64, jnp.sum(sums[0]), jnp.sum(sums[1]))
        both = jnp.where(lane == 126, jnp.sum(sums[2]), both)
        rows_out[...] = jnp.where(lane == 127, excess, both)


def plan_sends(neighbours, me, lists, step):
    bricks = neighbours.shape[0]
    low = me * bricks
    high = low + bricks
    following = (me & 1) * 128
    preceding = 128 - following

    def brick(b, counts):
        ahead, behind = counts
        near = [neighbours[b, c] for c in range(18)]
        held = [jnp.where(v < 0, 1 << 30, v) for v in near]
        for face in range(6):
            columns = [c for c in range(18) if GIVEN[c] == face]
            last = functools.reduce(jnp.maximum, [near[c] for c in columns])
            first = functools.reduce(jnp.minimum, [held[c] for c in columns])
            lists[following + ahead] = b * 6 + face
            lists[preceding + behind] = b * 6 + face
            ahead += jnp.where(last >= high, 1, 0)
            behind += jnp.where(first < low, 1, 0)
        return ahead, behind

    @pl.when(step == 0)
    def _():
        lists[127] = 0
        lists[255] = 0

    start = step * GROUP
    ahead, behind = lax.fori_loop(start, jnp.minimum(start + GROUP, bricks), brick,
                                  (lists[following + 127], lists[preceding + 127]))
    lists[following + 127] = ahead
    lists[preceding + 127] = behind


def select_blocks(lists, table, send):
    slots = send[0].shape[0]

    @pl.when(pl.program_id(0) == pl.num_programs(0) - 1)
    def _():
        def slot(s, carry):
            for partner in range(2):
                listed = s < lists[128 * partner + 127]
                send[partner][s] = table[jnp.where(listed, lists[128 * partner + s], 0)]
            return carry

        lax.fori_loop(0, slots, slot, 0, unroll=4)


def outlet_mark(kinds):
    def mark(chunk):
        start = 128 * chunk
        if not isinstance(start, int):
            start = pl.multiple_of(start, 128)
        return jnp.where(kinds[:, pl.ds(start, 128)] == 3, 1.0, 0.0)

    return mark


def first_kernel(bricks, me, neighbours, pops, kinds, posted, faces, send_even, send_odd, rows_out, lists,
                 layers, sums):
    step = pl.program_id(0)
    slots = send_even.shape[0]

    plan_sends(neighbours, me[0], lists, step)
    excess = jnp.where(jnp.maximum(lists[127], lists[255]) > slots, 1.0, 0.0)

    def load(i, c):
        return pops[i, :, pl.ds(pl.multiple_of(128 * c, 128), 128)]

    collide_all(load, kinds, posted, sums, rows_out, step, bricks, excess)
    pack(lambda m, c: posted[0, m, c], outlet_mark(kinds), layers, faces, step)
    select_blocks(lists, faces, (send_even, send_odd))


def take_table(pieces, table, sems):
    copies = []
    start = 0
    for k, piece in enumerate(pieces):
        count = piece.shape[0]
        copies.append(pltpu.make_async_copy(piece, table.at[pl.ds(start, count)], sems.at[k]))
        start += count
    for copy in copies:
        copy.start()
    for copy in copies:
        copy.wait()


def middle_kernel(bricks, lists, index, gathered, before, kinds, absent, own, even, odd,
                  posted, faces, send_even, send_odd, rows_out, table, arriving, pops, layers, sums, sems):
    step = pl.program_id(0)

    @pl.when(step == 0)
    def _():
        take_table((own, even, odd), table, sems)

    mean = mean_of(gathered)
    gather(bricks, index, step, gathered, table, mean, arriving)

    def put(member, chunk, value):
        pops[member, chunk] = value

    stream(before, kinds, absent, arriving, mean, put)
    collide_all(lambda i, c: pops[i, c], kinds, posted, sums, rows_out, step, bricks, 0.0)
    pack(lambda m, c: posted[0, m, c], outlet_mark(kinds), layers, faces, step)
    select_blocks(lists, faces, (send_even, send_odd))


def last_kernel(bricks, index, gathered, before, kinds, absent, own, even, odd, out, table, arriving, sems):
    step = pl.program_id(0)

    @pl.when(step == 0)
    def _():
        take_table((own, even, odd), table, sems)

    mean = mean_of(gathered)
    gather(bricks, index, step, gathered, table, mean, arriving)

    def put(member, chunk, value):
        start = 128 * chunk
        if not isinstance(start, int):
            start = pl.multiple_of(start, 128)
        out[member, :, pl.ds(start, 128)] = value

    stream(before, kinds, absent, arriving, mean, put)


F32 = jnp.float32
BLOCK = (BRICK, 128)
POSTED = (19, CHUNKS, GROUP, 128)


def params():
    return pltpu.CompilerParams(
        dimension_semantics=("arbitrary",), vmem_limit_bytes=LIMIT * 1024 * 1024)


def whole(*shape):
    return pl.BlockSpec(shape, lambda i: (0,) * len(shape))


SPEC_POPS = pl.BlockSpec((19, GROUP, SITES), lambda i: (0, i, 0))
SPEC_KINDS = pl.BlockSpec((GROUP, SITES), lambda i: (i, 0))
SPEC_POSTED = pl.BlockSpec((1,) + POSTED, lambda i: (i, 0, 0, 0, 0))
SPEC_ABSENT = pl.BlockSpec((18, GROUP, 128), lambda i: (0, i, 0))
SPEC_SMEM = pl.BlockSpec(memory_space=pltpu.SMEM)
SPEC_ANY = pl.BlockSpec(memory_space=pl.ANY)


def shape_of(*shape):
    return jax.ShapeDtypeStruct(shape, F32)


def first_call(slots, me, neighbours, pops, kinds, groups, devices):
    blocks = groups * GROUP * 6
    return pl.pallas_call(
        functools.partial(first_kernel, pops.shape[1]),
        grid=(groups,),
        in_specs=[SPEC_SMEM, SPEC_SMEM, SPEC_POPS, SPEC_KINDS],
        out_specs=[SPEC_POSTED, whole(blocks, *BLOCK), whole(slots, *BLOCK), whole(slots, *BLOCK),
                   whole(devices, 128), SPEC_SMEM],
        out_shape=[shape_of(groups, *POSTED), pltpu.HBM((blocks,) + BLOCK, F32), shape_of(slots, *BLOCK),
                   shape_of(slots, *BLOCK), shape_of(devices, 128),
                   jax.ShapeDtypeStruct((256,), jnp.int32)],
        scratch_shapes=[pltpu.VMEM((6, 128, 128), F32), pltpu.VMEM((3, GROUP, 128), F32)],
        compiler_params=params(),
        name="first_collide",
    )(me, neighbours, pops, kinds)


def middle_call(bricks, slots, lists, index, gathered, before, kinds, absent, tables, groups, devices):
    blocks = groups * GROUP * 6
    return pl.pallas_call(
        functools.partial(middle_kernel, bricks),
        grid=(groups,),
        in_specs=[SPEC_SMEM, SPEC_SMEM, whole(devices, 128), SPEC_POSTED, SPEC_KINDS,
                  SPEC_ABSENT] + [SPEC_ANY] * 3,
        out_specs=[SPEC_POSTED, whole(blocks, *BLOCK), whole(slots, *BLOCK), whole(slots, *BLOCK),
                   whole(devices, 128)],
        out_shape=[shape_of(groups, *POSTED), pltpu.HBM((blocks,) + BLOCK, F32), shape_of(slots, *BLOCK),
                   shape_of(slots, *BLOCK), shape_of(devices, 128)],
        scratch_shapes=[pltpu.VMEM((blocks + 2 * slots,) + BLOCK, F32),
                        pltpu.VMEM((18, 128, 128), F32), pltpu.VMEM(POSTED, F32),
                        pltpu.VMEM((6, 128, 128), F32), pltpu.VMEM((3, GROUP, 128), F32),
                        pltpu.SemaphoreType.DMA((3,))],
        compiler_params=params(),
        name="arrive_collide",
    )(lists, index, gathered, before, kinds, absent, *tables)


def last_call(bricks, slots, index, gathered, before, kinds, absent, tables, groups, devices):
    blocks = groups * GROUP * 6
    return pl.pallas_call(
        functools.partial(last_kernel, bricks),
        grid=(groups,),
        in_specs=[SPEC_SMEM, whole(devices, 128), SPEC_POSTED, SPEC_KINDS, SPEC_ABSENT] + [SPEC_ANY] * 3,
        out_specs=SPEC_POPS,
        out_shape=shape_of(19, bricks, SITES),
        scratch_shapes=[pltpu.VMEM((blocks + 2 * slots,) + BLOCK, F32),
                        pltpu.VMEM((18, 128, 128), F32), pltpu.SemaphoreType.DMA((3,))],
        compiler_params=params(),
        name="arrive_out",
    )(index, gathered, before, kinds, absent, *tables)


def share_sums(rows):
    return lax.all_to_all(rows, AXES, 0, 0, tiled=True)


def swap(send, devices):
    even_pairs = [(i, i ^ 1) for i in range(devices)]
    odd_pairs = [(i, i + 1) for i in range(1, devices - 1, 2)]
    odd_pairs = odd_pairs + [(b, a) for a, b in odd_pairs]
    return lax.ppermute(send[0], AXES, even_pairs), lax.ppermute(send[1], AXES, odd_pairs)


def rank(used):
    count = used.shape[0]
    return jnp.sum(jnp.where(iota((count, count), 1) < iota((count, count), 0), used[None, :], 0), axis=1)


def arrival_plan(neighbours, slots, padded):
    bricks = neighbours.shape[0]
    blocks = bricks * 6
    me = lax.axis_index(AXES)
    local = neighbours - me * bricks
    present = neighbours >= 0
    following = present & (local >= bricks)
    preceding = present & (local < 0)
    first = me % 2 == 0
    read = jnp.asarray(np.array(COLUMN_FACE, np.int32))
    index = local * 6 + read[None, :]
    for partner in range(2):
        is_next = first if partner == 0 else ~first
        there = jnp.where(is_next, following, preceding)
        spot = (local + jnp.where(is_next, -bricks, bricks)) * 6 + read[None, :]
        flat = jnp.where(there, spot, -1).reshape(-1)
        hits = flat[:, None] == iota((flat.shape[0], blocks), 1)
        ranks = rank(jnp.any(hits, axis=0).astype(jnp.int32))
        at = jnp.sum(jnp.where(hits, jnp.minimum(ranks, slots - 1)[None, :], 0), axis=1)
        index = jnp.where(there, padded * 6 + partner * slots + at.reshape(bricks, 18), index)
    index = jnp.where(present, index, 0)
    index = jnp.pad(index, ((0, padded - bricks), (0, 0))).reshape(-1)
    return jnp.concatenate([index, me[None]])


def begin(devices, slots, populations, neighbours, site_flags, absent):
    bricks = populations.shape[1]
    groups = absent.shape[1] // GROUP
    me = lax.axis_index(AXES).astype(jnp.int32).reshape(1)
    index = arrival_plan(neighbours, slots, groups * GROUP)
    posted, faces, *send, rows, lists = first_call(
        slots, me, neighbours, populations, site_flags, groups, devices)
    gathered = share_sums(rows)
    sent = swap(send, devices)
    excess = jnp.sum(gathered[:, 127])
    posted, faces, *send, rows = middle_call(
        bricks, slots, lists, index, gathered, posted, site_flags, absent,
        (faces,) + sent, groups, devices)
    gathered = share_sums(rows)
    sent = swap(send, devices)
    return excess, (index, gathered, posted, faces) + sent


def finish(devices, slots, site_flags, absent, bricks, state):
    index, gathered, posted = state[:3]
    return last_call(bricks, slots, index, gathered, posted, site_flags, absent,
                     state[3:], absent.shape[1] // GROUP, devices)


def on_device(devices, populations, neighbours, site_flags):
    bricks = populations.shape[0]
    padded = -(-bricks // GROUP) * GROUP
    absent = jnp.pad((neighbours < 0).astype(jnp.int32), ((0, padded - bricks), (0, 0)))
    absent = jnp.broadcast_to(absent.T[:, :, None], (18, padded, 128))
    populations = jnp.transpose(populations, (1, 0, 2))
    excess, state = begin(devices, SLOTS, populations, neighbours, site_flags, absent)

    def enough(populations, neighbours, state):
        return finish(devices, SLOTS, site_flags, absent, bricks, state)

    def too_few(populations, neighbours, state):
        every = bricks * 6
        _, state = begin(devices, every, populations, neighbours, site_flags, absent)
        return finish(devices, every, site_flags, absent, bricks, state)

    out = lax.cond(excess > 0.0, too_few, enough, populations, neighbours, state)
    return jnp.transpose(out, (1, 0, 2))


def solution(mesh):
    devices = mesh.shape["seg"] * mesh.shape["sub"]
    in_specs = (P(AXES, None, None), P(AXES, None), P(AXES, None))
    return jax.shard_map(
        functools.partial(on_device, devices), mesh=mesh, in_specs=in_specs,
        out_specs=P(AXES, None, None), check_vma=False)
```
